32 devices in a mesh: group: 2 (over y), row: 4 (over z), col: 4 (over x, core).
Axes of the slice: x: 2, y: 2, z: 4, core: 2. Of those that a mesh axis runs over, the one named last changes fastest.
Arguments:
- features: bfloat16 [65536, 128], P(('group', 'row', 'col')), parts along dimension 0, may hold values from -6 to 6
- cotangent: bfloat16 [65536, 128], P(('group', 'row', 'col')), parts along dimension 0, may hold values from -6 to 6
- fine_weight: bfloat16 [128, 128], replicated, may hold values from -0.5 to 0.5
- middle_weight: bfloat16 [128, 128], replicated, may hold values from -0.5 to 0.5
- top_weight: bfloat16 [128, 128], replicated, may hold values from -0.5 to 0.5
- tile_bank: bfloat16 [32, 128, 128], replicated, may hold values from -0.25 to 0.25
- fine_source: int32 [4096], P(('group', 'row', 'col')), parts along dimension 0, may hold values from 0 to 23
- fine_target: int32 [4096], P(('group', 'row', 'col')), parts along dimension 0, may hold values from 0 to 15
- fine_kind: int32 [4096], P(('group', 'row', 'col')), parts along dimension 0, may hold values from 0 to 31
- tile_count: int32 [32], P(('group', 'row', 'col')), parts along dimension 0, may hold values from 25 to 128, as said below
- fine_sends: int32 [256], P(('group', 'row', 'col')), parts along dimension 0, may hold values from 0 to 15
- fine_pool: int32 [65536], P(('group', 'row', 'col')), parts along dimension 0, may hold values from 0 to 1023
- middle_source: int32 [256], P(('group', 'row')), parts along dimension 0, may hold values from 0 to 11
- middle_target: int32 [256], P(('group', 'row')), parts along dimension 0, may hold values from 0 to 7
- middle_kind: int32 [256], P(('group', 'row')), parts along dimension 0, may hold values from 0 to 31
- middle_sends: int32 [32], P(('group', 'row')), parts along dimension 0, may hold values from 0 to 7
- middle_pool: int32 [8192], P(('group', 'row')), parts along dimension 0, may hold values from 0 to 511
- top_source: int32 [32], P('group'), parts along dimension 0, may hold values from 0 to 3
- top_kind: int32 [32], P('group'), parts along dimension 0, may hold values from 0 to 31
Outputs:
- fine_out: bfloat16 [65536, 128], P(('group', 'row', 'col')), parts along dimension 0
- grad_features: bfloat16 [65536, 128], P(('group', 'row', 'col')), parts along dimension 0
- weight_grads: float32 [6, 128, 128], P('group'), parts along dimension 0
The draws below stay inside these ranges and needn't reach their ends.
There are 2 independent parts, one for each index of `group`. The reference program is written for one: setup_inputs(seed, part) draws one part's arguments, and reference() takes and returns one part's arrays. A program takes and returns all parts, laid end to end along the dimension named above; an argument that names none is the same for every part. Nothing has to cross between parts.
Inputs may be any that keep to these rules, and one draw needn't show every extreme that they name: Only the first tile_count[p] tile slots of partition p are live; later slots are ignored.
All inputs are finite; a program needn't handle non-finite values.
Results may differ from the reference program's by a relative error of at most 0.028.
Values may be sent and summed in bfloat16 or wider, within the bound.
A program may use at most 64 MiB of HBM per device.

```python
import jax
import jax.numpy as jnp
from jax import lax

H = 128
BS = 128
KINDS = 32
B1 = 16
SEND = 2
B2 = 8
SEND2 = 2
T3 = 4
T1 = 128
T2 = 32
NDEV = 16
N1 = 32768
N2R = 1024
N2 = 4096
N3 = 512
NT1 = 2048
NT2 = 128
NT3 = 16
N_ROW = 4
N_COL = 4


def draw_tile_count(key, part):
    key = jax.random.fold_in(key, 11)
    key_share, key_first, key_second = jax.random.split(key, 3)
    divisor = jax.random.randint(key_share, (NDEV,), 1, 6)
    counts = T1 // divisor
    first = jax.random.randint(key_first, (), 0, NDEV)
    second = (first + jax.random.randint(key_second, (), 1, NDEV)) % NDEV
    counts = counts.at[first].set(T1).at[second].set(T1 // 5)
    return counts.astype(jnp.int32)


def with_ends(entries, key, least, top_value):
    dims = entries.shape
    index_at = [jax.random.randint(jax.random.fold_in(key, axis), (), 0, dims[axis]) for axis in range(len(dims))]
    entries = entries.at[tuple(index_at)].set(least)
    longest = dims.index(max(dims))
    index_at[longest] = (index_at[longest] + 1) % dims[longest]
    return entries.at[tuple(index_at)].set(top_value)


def level_of(rng, shape, pieces, smallest, top_value):
    factor_of, own = 1.0, jax.random.fold_in(rng, 6)
    for dim, shards_of in pieces:
        heights = jnp.exp(jax.random.uniform(jax.random.fold_in(own, dim), (shards_of,), jnp.float32, smallest / len(pieces), top_value / len(pieces)))
        factor_of = factor_of * jnp.repeat(heights, shape[dim] // shards_of).reshape([-1 if axis == dim else 1 for axis in range(len(shape))])
    return factor_of


def normal_values(key, shape, scale, bound, cuts=(), kind=jnp.bfloat16):
    entries = scale * jax.random.normal(key, shape, jnp.float32)
    if cuts:
        entries = entries * level_of(key, shape, cuts, -0.22, 0.18)
    return jnp.clip(entries, -bound, bound).astype(kind)


def setup_inputs(seed: int = 0, part: int = 0) -> dict:
    streams_of = jax.random.split(jax.random.key(seed), 20)
    part_splits = jax.random.split(jax.random.fold_in(streams_of[19], part), 20)
    features = normal_values(part_splits[0], (N1, H), 1.0, 6.0, ((0, 16),))
    cotangent = normal_values(part_splits[1], (N1, H), 1.0, 6.0, ((0, 16),))
    fine_weight = normal_values(streams_of[2], (H, H), H ** -0.5, 0.5)
    middle_weight = normal_values(streams_of[3], (H, H), H ** -0.5, 0.5)
    top_weight = normal_values(streams_of[4], (H, H), H ** -0.5, 0.5)
    tile_bank = normal_values(streams_of[5], (KINDS, BS, BS), (4 * BS) ** -0.5, 0.25)
    fine_source = with_ends(jax.random.randint(part_splits[6], (NT1,), 0, B1 + 4 * SEND), jax.random.fold_in(part_splits[6], 1), 0, (B1 + 4 * SEND) - 1).astype(jnp.int32)
    fine_target = with_ends(jax.random.randint(part_splits[7], (NT1,), 0, B1), jax.random.fold_in(part_splits[7], 1), 0, B1 - 1).astype(jnp.int32)
    fine_kind = with_ends(jax.random.randint(part_splits[8], (NT1,), 0, KINDS), jax.random.fold_in(part_splits[8], 1), 0, KINDS - 1).astype(jnp.int32)
    tile_count = draw_tile_count(jax.random.fold_in(jax.random.fold_in(streams_of[19], part), 71), part)
    fine_sends = with_ends(jax.random.randint(part_splits[10], (NDEV * 4 * SEND,), 0, B1), jax.random.fold_in(part_splits[10], 1), 0, B1 - 1).astype(jnp.int32)
    fine_pool = with_ends(jax.random.randint(part_splits[11], (N1,), 0, N2R), jax.random.fold_in(part_splits[11], 1), 0, N2R - 1).astype(jnp.int32)
    middle_source = with_ends(jax.random.randint(part_splits[12], (NT2,), 0, B2 + 2 * SEND2), jax.random.fold_in(part_splits[12], 1), 0, (B2 + 2 * SEND2) - 1).astype(jnp.int32)
    middle_target = with_ends(jax.random.randint(part_splits[13], (NT2,), 0, B2), jax.random.fold_in(part_splits[13], 1), 0, B2 - 1).astype(jnp.int32)
    middle_kind = with_ends(jax.random.randint(part_splits[14], (NT2,), 0, KINDS), jax.random.fold_in(part_splits[14], 1), 0, KINDS - 1).astype(jnp.int32)
    middle_sends = with_ends(jax.random.randint(part_splits[15], (N_ROW * 2 * SEND2,), 0, B2), jax.random.fold_in(part_splits[15], 1), 0, B2 - 1).astype(jnp.int32)
    middle_pool = with_ends(jax.random.randint(part_splits[16], (N2,), 0, N3), jax.random.fold_in(part_splits[16], 1), 0, N3 - 1).astype(jnp.int32)
    top_source = with_ends(jax.random.randint(part_splits[17], (NT3,), 0, N_COL), jax.random.fold_in(part_splits[17], 1), 0, N_COL - 1).astype(jnp.int32)
    top_kind = with_ends(jax.random.randint(part_splits[18], (NT3,), 0, KINDS), jax.random.fold_in(part_splits[18], 1), 0, KINDS - 1).astype(jnp.int32)
    return dict(features=features, cotangent=cotangent, fine_weight=fine_weight, middle_weight=middle_weight, top_weight=top_weight, tile_bank=tile_bank, fine_source=fine_source, fine_target=fine_target, fine_kind=fine_kind, tile_count=tile_count, fine_sends=fine_sends, fine_pool=fine_pool, middle_source=middle_source, middle_target=middle_target, middle_kind=middle_kind, middle_sends=middle_sends, middle_pool=middle_pool, top_source=top_source, top_kind=top_kind)


tile_group = 8

def gelu_slope(value):
    return jax.vjp(jax.nn.gelu, value)[1](jnp.ones_like(value))[0]

def shift_grid(field, axis, step):
    zeros = jnp.zeros_like(lax.slice_in_dim(field, 0, 1, axis=axis))
    length = field.shape[axis]
    if step > 0:
        return jnp.concatenate([zeros, lax.slice_in_dim(field, 0, length - 1, axis=axis)], axis)
    return jnp.concatenate([lax.slice_in_dim(field, 1, length, axis=axis), zeros], axis)

def tile_forward(bank, kinds, sources, targets, live, extended, blocks):
    count = kinds.shape[0]
    group = min(tile_group, count)

    def add_group(total, index):
        start = index * group
        kind_part = lax.dynamic_slice_in_dim(kinds, start, group)
        source_part = lax.dynamic_slice_in_dim(sources, start, group)
        target_part = lax.dynamic_slice_in_dim(targets, start, group)
        live_part = lax.dynamic_slice_in_dim(live, start, group)
        tiles = bank[kind_part].astype(jnp.float32)
        inputs = extended[source_part].astype(jnp.float32)
        products = jnp.einsum('tij,tjh->tih', tiles, inputs, precision=lax.Precision.HIGHEST)
        products = products * live_part.astype(jnp.float32)[:, None, None]
        return (total.at[target_part].add(products), None)
    initial = jnp.zeros((blocks,) + extended.shape[1:], jnp.float32)
    total, unused = lax.scan(add_group, initial, jnp.arange(count // group, dtype=jnp.int32))
    return total

def tile_backward(bank, kinds, sources, targets, live, grads, extent):
    count = kinds.shape[0]
    group = min(tile_group, count)

    def add_group(total, index):
        start = index * group
        kind_part = lax.dynamic_slice_in_dim(kinds, start, group)
        source_part = lax.dynamic_slice_in_dim(sources, start, group)
        target_part = lax.dynamic_slice_in_dim(targets, start, group)
        live_part = lax.dynamic_slice_in_dim(live, start, group)
        tiles = bank[kind_part].astype(jnp.float32)
        inputs = grads[target_part].astype(jnp.float32)
        products = jnp.einsum('tji,tjh->tih', tiles, inputs, precision=lax.Precision.HIGHEST)
        products = products * live_part.astype(jnp.float32)[:, None, None]
        return (total.at[source_part].add(products), None)
    initial = jnp.zeros((extent,) + grads.shape[1:], jnp.float32)
    total, unused = lax.scan(add_group, initial, jnp.arange(count // group, dtype=jnp.int32))
    return total

def reference(features, cotangent, fine_weight, middle_weight, top_weight, tile_bank, fine_source, fine_target, fine_kind, tile_count, fine_sends, fine_pool, middle_source, middle_target, middle_kind, middle_sends, middle_pool, top_source, top_kind):
    partitions = N_ROW * N_COL
    own_rows = B1 * BS
    pool_two = (N2R / (own_rows * N_COL)) ** 0.5
    pool_three = (N3 / (N2R * N_ROW)) ** 0.5
    pick = jax.vmap(lambda table, index: table[index])
    add_back = jax.vmap(lambda table, index, values: table.at[index].add(values))
    fine_message = jnp.dot(features, fine_weight, preferred_element_type=jnp.float32).astype(jnp.bfloat16)
    fine_blocks = fine_message.reshape(partitions, B1, BS, H)
    sends = fine_sends.reshape(partitions, 4 * SEND)
    outgoing = pick(fine_blocks, sends).reshape(N_ROW, N_COL, 4, SEND, BS, H)
    received = jnp.concatenate([shift_grid(outgoing[:, :, 0], 0, 1), shift_grid(outgoing[:, :, 1], 0, -1), shift_grid(outgoing[:, :, 2], 1, 1), shift_grid(outgoing[:, :, 3], 1, -1)], 2)
    fine_extended = jnp.concatenate([fine_blocks, received.reshape(partitions, 4 * SEND, BS, H)], 1)
    live_fine = jnp.arange(T1, dtype=jnp.int32)[None, :] < tile_count[:, None]
    kinds = fine_kind.reshape(partitions, T1)
    sources = fine_source.reshape(partitions, T1)
    targets = fine_target.reshape(partitions, T1)
    fine_summed = jax.vmap(lambda k, s, d, l, e: tile_forward(tile_bank, k, s, d, l, e, B1))(kinds, sources, targets, live_fine, fine_extended).reshape(N1, H)
    fine_hidden = features.astype(jnp.float32) + jax.nn.gelu(fine_summed)
    row_pool = fine_pool.reshape(N_ROW, N_COL * own_rows)
    row_sum = jax.vmap(lambda values, index: jax.ops.segment_sum(values, index, num_segments=N2R))
    coarse = row_sum(fine_hidden.reshape(N_ROW, N_COL * own_rows, H), row_pool) * pool_two
    coarse_low = coarse.reshape(N2, H).astype(jnp.bfloat16)
    middle_message = jnp.dot(coarse_low, middle_weight, preferred_element_type=jnp.float32).astype(jnp.bfloat16)
    middle_blocks = middle_message.reshape(N_ROW, B2, BS, H)
    middle_list = middle_sends.reshape(N_ROW, 2 * SEND2)
    middle_out = pick(middle_blocks, middle_list).reshape(N_ROW, 2, SEND2, BS, H)
    middle_received = jnp.concatenate([shift_grid(middle_out[:, 0], 0, 1), shift_grid(middle_out[:, 1], 0, -1)], 1)
    middle_extended = jnp.concatenate([middle_blocks, middle_received], 1)
    live_middle = jnp.ones((N_ROW, T2), bool)
    middle_kinds = middle_kind.reshape(N_ROW, T2)
    middle_sources = middle_source.reshape(N_ROW, T2)
    middle_targets = middle_target.reshape(N_ROW, T2)
    middle_summed = jax.vmap(lambda k, s, d, l, e: tile_forward(tile_bank, k, s, d, l, e, B2))(middle_kinds, middle_sources, middle_targets, live_middle, middle_extended).reshape(N2, H)
    middle_hidden = coarse.reshape(N2, H) + jax.nn.gelu(middle_summed)
    top_state = jax.ops.segment_sum(middle_hidden, middle_pool, num_segments=N3) * pool_three
    top_low = top_state.astype(jnp.bfloat16)
    top_message = jnp.dot(top_low, top_weight, preferred_element_type=jnp.float32).astype(jnp.bfloat16)
    top_targets = jnp.arange(N_COL * T3, dtype=jnp.int32) // T3
    live_top = jnp.ones((N_COL * T3,), bool)
    top_summed = tile_forward(tile_bank, top_kind, top_source, top_targets, live_top, top_message.reshape(N_COL, BS, H), N_COL).reshape(N3, H)
    top_hidden = top_state + jax.nn.gelu(top_summed)
    middle_unpooled = middle_hidden + pool_three * top_hidden[middle_pool]
    spread = pick(middle_unpooled.reshape(N_ROW, N2R, H), row_pool).reshape(N1, H)
    fine_out = (fine_hidden + pool_two * spread).astype(jnp.bfloat16)
    grad_out = cotangent.astype(jnp.float32)
    grad_middle_sum = (row_sum(grad_out.reshape(N_ROW, N_COL * own_rows, H), row_pool) * pool_two).reshape(N2, H)
    grad_top_state = jax.ops.segment_sum(grad_middle_sum, middle_pool, num_segments=N3) * pool_three
    grad_top_summed = (grad_top_state * gelu_slope(top_summed)).astype(jnp.bfloat16)
    grad_top_message = tile_backward(tile_bank, top_kind, top_source, top_targets, live_top, grad_top_summed.reshape(N_COL, BS, H), N_COL).reshape(N3, H).astype(jnp.bfloat16)
    top_grad = jnp.dot(top_low.T, grad_top_message, preferred_element_type=jnp.float32)
    grad_top_full = grad_top_state + jnp.dot(grad_top_message, top_weight.T, preferred_element_type=jnp.float32)
    grad_middle_hidden = grad_middle_sum + pool_three * grad_top_full[middle_pool]
    grad_middle_summed = (grad_middle_hidden * gelu_slope(middle_summed)).astype(jnp.bfloat16).reshape(N_ROW, B2, BS, H)
    middle_terms = jax.vmap(lambda k, s, d, l, g: tile_backward(tile_bank, k, s, d, l, g, B2 + 2 * SEND2))(middle_kinds, middle_sources, middle_targets, live_middle, grad_middle_summed)
    middle_returned = jnp.concatenate([shift_grid(middle_terms[:, B2:B2 + SEND2], 0, -1), shift_grid(middle_terms[:, B2 + SEND2:], 0, 1)], 1)
    grad_middle_message = add_back(middle_terms[:, :B2], middle_list, middle_returned).reshape(N2, H).astype(jnp.bfloat16)
    middle_grad = jnp.dot(coarse_low.T, grad_middle_message, preferred_element_type=jnp.float32)
    grad_coarse = grad_middle_hidden + jnp.dot(grad_middle_message, middle_weight.T, preferred_element_type=jnp.float32)
    grad_fine_hidden = grad_out + pool_two * pick(grad_coarse.reshape(N_ROW, N2R, H), row_pool).reshape(N1, H)
    grad_fine_summed = (grad_fine_hidden * gelu_slope(fine_summed)).astype(jnp.bfloat16).reshape(partitions, B1, BS, H)
    fine_terms = jax.vmap(lambda k, s, d, l, g: tile_backward(tile_bank, k, s, d, l, g, B1 + 4 * SEND))(kinds, sources, targets, live_fine, grad_fine_summed)
    grid_terms = fine_terms.reshape(N_ROW, N_COL, B1 + 4 * SEND, BS, H)

    def segment(number):
        return grid_terms[:, :, B1 + number * SEND:B1 + (number + 1) * SEND]
    returned = jnp.concatenate([shift_grid(segment(0), 0, -1), shift_grid(segment(1), 0, 1), shift_grid(segment(2), 1, -1), shift_grid(segment(3), 1, 1)], 2)
    grad_fine_message = add_back(fine_terms[:, :B1], sends, returned.reshape(partitions, 4 * SEND, BS, H))
    grad_fine_message = grad_fine_message.reshape(N1, H).astype(jnp.bfloat16)
    fine_grad = jnp.dot(features.T, grad_fine_message, preferred_element_type=jnp.float32)
    grad_features = (grad_fine_hidden + jnp.dot(grad_fine_message, fine_weight.T, preferred_element_type=jnp.float32)).astype(jnp.bfloat16)
    scales = jnp.array([N1 ** (-0.5), N2 ** (-0.5), N3 ** (-0.5)], jnp.float32)
    weight_grads = jnp.stack([fine_grad, middle_grad, top_grad]) * scales[:, None, None]
    return (fine_out, grad_features, weight_grads)
```

```python
import functools

import jax
import jax.numpy as jnp
from jax import lax
from jax.experimental import pallas as pl
from jax.experimental.pallas import tpu as pltpu
from jax.sharding import PartitionSpec as P

MESH = pl.DeviceIdType.MESH
F32 = jnp.float32
BF16 = jnp.bfloat16
UNROLL = 8


def gelu_pair(x):
    k = 0.7978845608028654
    a = 0.044715
    square = x * x
    t = jnp.tanh(k * (x + a * (square * x)))
    half = 0.5 + 0.5 * t
    slope = half + (0.5 * k) * x * ((1.0 - t * t) * (1.0 + (3.0 * a) * square))
    return x * half, slope


def mm(a, b):
    return jnp.dot(a, b, preferred_element_type=F32)


def mm_tn(a, b):
    return lax.dot_general(a, b, (((0,), (0,)), ((), ())), preferred_element_type=F32)


def mm_nt(a, b):
    return lax.dot_general(a, b, (((1,), (1,)), ((), ())), preferred_element_type=F32)


def loop(count, body, unroll=1):
    while count % unroll:
        unroll //= 2

    def step(index, carry):
        for inner in range(unroll):
            body(index * unroll + inner)
        return carry

    lax.fori_loop(0, count // unroll, step, 0)


def kernel(
    dims,
    prev,
    last,
    fine_source,
    fine_target,
    fine_kind,
    fine_sends,
    middle_source,
    middle_target,
    middle_kind,
    middle_sends,
    top_source,
    top_kind,
    feat,
    cot,
    w_fine,
    w_middle,
    w_top,
    bank,
    fine_pool,
    middle_pool,
    fine_out,
    grad_out,
    weight_out,
    bank_t,
    pool_map,
    pick_map,
    chain,
    ext,
    send_fine,
    back_fine,
    home_fine,
    hidden,
    slope,
    grad_hidden,
    grad_sum,
    grad_blocks,
    part_h,
    part_g,
    slots_h,
    slots_g,
    full_h,
    full_g,
    m_ext,
    m_send,
    m_back,
    m_home,
    m_hidden,
    m_slope,
    m_grad,
    m_low,
    m_gsum,
    m_gmsg,
    table,
    top_slots_h,
    top_slots_g,
    top_h,
    top_g,
    t_msg,
    t_gsum,
    t_slope,
    t_gmsg,
    t_table,
    mg_slots,
    fg_slots_col,
    fg_slots_row,
    send_sem,
    recv_sem,
):
    n_row, n_col, send, m_send_n, t_slots = dims
    r = lax.axis_index("row")
    c = lax.axis_index("col")
    place = {"row": (r, n_row), "col": (c, n_col)}
    kinds, bs, width = bank.shape
    rows = feat.shape[0]
    blocks = rows // bs
    m_rows = m_low.shape[0]
    m_blocks = m_rows // bs
    t_rows = n_col * bs
    chunk = m_rows // n_col
    p2 = (m_rows / (rows * n_col)) ** 0.5
    p3 = (t_rows / (m_rows * n_row)) ** 0.5
    allotted = [0]

    def semaphores(count):
        base = allotted[0]
        allotted[0] += count
        return base

    def remote(src, dst, s, v, axis, target):
        return pltpu.make_async_remote_copy(
            src_ref=src,
            dst_ref=dst,
            send_sem=send_sem.at[s],
            recv_sem=recv_sem.at[v],
            device_id={axis: target},
            device_id_type=MESH,
        )

    class Exchange:
        def __init__(self, source, slots, axis):
            self.source, self.slots, self.axis = source, slots, axis
            self.me, self.n = place[axis]
            self.base = semaphores(self.n)

        def start(self):
            for k in range(1, self.n):
                p = lax.rem(self.me + k, self.n)
                remote(
                    self.source(p),
                    self.slots.at[self.me],
                    self.base + k,
                    self.base + self.me,
                    self.axis,
                    p,
                ).start()

        def wait(self):
            for k in range(1, self.n):
                p = lax.rem(self.me + k, self.n)
                remote(
                    self.source(p),
                    self.slots.at[p],
                    self.base + k,
                    self.base + p,
                    self.axis,
                    p,
                ).wait()

        def total(self):
            value = self.slots[0].astype(F32)
            for k in range(1, self.n):
                value = value + self.slots[k].astype(F32)
            return value

    class Shift:
        def __init__(self, source, target, axis, delta):
            self.me, self.n = place[axis]
            self.base = semaphores(1)
            self.copy = lambda p: remote(source, target, self.base, self.base, axis, p)
            self.delta = delta
            low, high = self.me > 0, self.me < self.n - 1
            self.sends, self.gets = (high, low) if delta > 0 else (low, high)
            self.lacks = jnp.logical_not(self.gets)
            self.target = target

        def clear(self):
            @pl.when(self.lacks)
            def _():
                self.target[...] = jnp.zeros(self.target.shape, BF16)

        def start(self):
            @pl.when(self.sends)
            def _():
                self.copy(self.me + self.delta).start()

        def wait(self):
            other = jnp.clip(self.me + self.delta, 0, self.n - 1)

            @pl.when(self.sends)
            def _():
                self.copy(other).wait_send()

            @pl.when(self.gets)
            def _():
                self.copy(other).wait_recv()

    ways = (("row", 1), ("row", -1), ("col", 1), ("col", -1))
    halo = [
        Shift(send_fine.at[k], ext.at[pl.ds(blocks + send * k, send)], axis, delta)
        for k, (axis, delta) in enumerate(ways)
    ]
    home = [
        Shift(back_fine.at[k], home_fine.at[k], axis, -delta)
        for k, (axis, delta) in enumerate(ways)
    ]
    m_halo = [
        Shift(
            m_send.at[k], m_ext.at[pl.ds(m_blocks + m_send_n * k, m_send_n)], axis, delta
        )
        for k, (axis, delta) in enumerate(ways[:2])
    ]
    m_homes = [
        Shift(m_back.at[k], m_home.at[k], axis, -delta)
        for k, (axis, delta) in enumerate(ways[:2])
    ]
    scatter_h = Exchange(lambda p: part_h.at[p], slots_h, "col")
    scatter_g = Exchange(lambda p: part_g.at[p], slots_g, "col")
    gather_h = Exchange(lambda p: full_h.at[c], full_h, "col")
    gather_g = Exchange(lambda p: full_g.at[c], full_g, "col")
    rows_h = Exchange(lambda p: top_slots_h.at[r], top_slots_h, "row")
    rows_g = Exchange(lambda p: top_slots_g.at[r], top_slots_g, "row")
    cols_h = Exchange(lambda p: top_h.at[c], top_h, "col")
    cols_g = Exchange(lambda p: top_g.at[c], top_g, "col")
    sum_middle = Exchange(lambda p: mg_slots.at[r], mg_slots, "row")
    sum_fine_col = Exchange(lambda p: fg_slots_col.at[c], fg_slots_col, "col")
    sum_fine_row = Exchange(lambda p: fg_slots_row.at[r], fg_slots_row, "row")

    barrier = pltpu.get_barrier_semaphore()
    for axis in ("row", "col"):
        me, n = place[axis]
        for k in range(1, n):
            pl.semaphore_signal(
                barrier, inc=1, device_id={axis: lax.rem(me + k, n)}, device_id_type=MESH
            )
    for item in halo + home + m_halo + m_homes:
        item.clear()
    chain[0] = jnp.zeros((bs, width), F32)

    def message(b):
        value = mm(feat[pl.ds(pl.multiple_of(b * bs, bs), bs), :], w_fine[...]).astype(BF16)
        ext[b] = value
        grad_blocks[b] = value

    loop(blocks, message, 4)
    for k in range(4):
        for i in range(send):
            send_fine[k, i] = grad_blocks[fine_sends[k * send + i]]
    pl.semaphore_wait(barrier, n_row + n_col - 2)
    for item in halo:
        item.start()

    def pool_block(j):
        index = fine_pool[pl.ds(j, 1), :]
        for i in range(m_blocks):
            ids = lax.broadcasted_iota(jnp.int32, (bs, bs), 0) + i * bs
            pool_map[i * bs : (i + 1) * bs, pl.ds(pl.multiple_of(j * bs, bs), bs)] = jnp.where(
                ids == index, 1.0, 0.0
            ).astype(BF16)

    loop(blocks, pool_block)

    def pool_into(part, values):
        def one(m):
            part[m] = mm(pool_map[pl.ds(pl.multiple_of(m * chunk, chunk), chunk), :], values[...]).astype(
                BF16
            )

        loop(n_col, one)

    pool_into(part_g, cot)
    slots_g[c] = part_g[c]
    scatter_g.start()

    def flip(k):
        bank_t[k] = bank[k].astype(F32).T.astype(BF16)

    loop(kinds, flip, 4)
    for item in halo:
        item.wait()
    scatter_g.wait()
    full_g[c] = scatter_g.total().astype(BF16)
    gather_g.start()

    def fine_slot(t):
        chain[t + 1] = mm(bank[fine_kind[t]], ext[fine_source[t]]) + chain[prev[0, t]]

    loop(fine_kind.shape[0], fine_slot, UNROLL)

    def fine_state(b):
        at = pl.ds(pl.multiple_of(b * bs, bs), bs)
        value, rate = gelu_pair(chain[last[0, b]])
        state = feat[at, :].astype(F32) + value
        hidden[at, :] = state
        slope[at, :] = rate
        grad_sum[at, :] = state.astype(BF16)

    loop(blocks, fine_state)
    pool_into(part_h, grad_sum)
    slots_h[c] = part_h[c]
    scatter_h.start()

    gather_g.wait()
    for k in range(n_col):
        m_gsum[k * chunk : (k + 1) * chunk, :] = full_g[k].astype(F32) * p2

    def top_partial(values):
        maps = []
        for j in range(m_blocks):
            ids = lax.broadcasted_iota(jnp.int32, (bs, bs), 0) + c * bs
            maps.append(jnp.where(ids == middle_pool[j : j + 1, :], 1.0, 0.0).astype(BF16))
        return mm(jnp.concatenate(maps, axis=1), values)

    top_slots_g[r] = top_partial(m_gsum[...].astype(BF16)).astype(BF16)
    rows_g.start()

    def pick_block(j):
        index = jnp.broadcast_to(fine_pool[pl.ds(j, 1), :].astype(F32), (bs, bs)).T
        for i in range(m_blocks):
            ids = (lax.broadcasted_iota(jnp.int32, (bs, bs), 1) + i * bs).astype(F32)
            pick_map[pl.ds(pl.multiple_of(j * bs, bs), bs), i * bs : (i + 1) * bs] = jnp.where(
                ids == index, 1.0, 0.0
            ).astype(BF16)

    scatter_h.wait()
    full_h[c] = scatter_h.total().astype(BF16)
    gather_h.start()
    loop(blocks, pick_block)
    rows_g.wait()
    top_g[c] = (rows_g.total() * p3).astype(BF16)
    cols_g.start()
    gather_h.wait()

    for k in range(n_col):
        at = slice(k * chunk, (k + 1) * chunk)
        value = full_h[k].astype(F32) * p2
        m_hidden[at, :] = value
        m_low[at, :] = value.astype(BF16)
    for b in range(m_blocks):
        value = mm(m_low[b * bs : (b + 1) * bs, :], w_middle[...]).astype(BF16)
        m_ext[b] = value
        m_grad[b] = value
    for k in range(2):
        for i in range(m_send_n):
            m_send[k, i] = m_grad[middle_sends[k * m_send_n + i]]
    for item in m_halo:
        item.start()
    cols_g.wait()
    for item in m_halo:
        item.wait()

    def middle_slot(t):
        chain[t + 1] = mm(bank[middle_kind[t]], m_ext[middle_source[t]]) + chain[prev[2, t]]

    loop(middle_kind.shape[0], middle_slot, UNROLL)

    def middle_state(b):
        at = pl.ds(pl.multiple_of(b * bs, bs), bs)
        value, rate = gelu_pair(chain[last[2, b]])
        m_hidden[at, :] = m_hidden[at, :] + value
        m_slope[at, :] = rate

    loop(m_blocks, middle_state)
    top_slots_h[r] = top_partial(m_hidden[...].astype(BF16)).astype(BF16)
    rows_h.start()
    rows_h.wait()
    top_h[c] = (rows_h.total() * p3).astype(BF16)
    cols_h.start()
    cols_h.wait()

    def top_message(b):
        t_msg[b] = mm(top_h[b], w_top[...]).astype(BF16)

    loop(n_col, top_message)

    def top_state(b):
        total = jnp.zeros((bs, width), F32)
        for s in range(t_slots):
            t = b * t_slots + s
            total = total + mm(bank[top_kind[t]], t_msg[top_source[t]])
        value, rate = gelu_pair(total)
        at = pl.ds(pl.multiple_of(b * bs, bs), bs)
        t_table[at, :width] = (top_h[b].astype(F32) + value).astype(BF16)
        t_gsum[b] = (top_g[b].astype(F32) * rate).astype(BF16)

    loop(n_col, top_state)

    def top_back(b):
        for s in range(t_slots):
            t = b * t_slots + s
            chain[t + 1] = mm(bank_t[top_kind[t]], t_gsum[b]) + chain[prev[4, t]]

    loop(n_col, top_back)

    def top_grad(b):
        at = pl.ds(pl.multiple_of(b * bs, bs), bs)
        message_grad = chain[last[4, b]].astype(BF16)
        t_gmsg[at, :] = message_grad
        t_table[at, width:] = (
            top_g[b].astype(F32) + mm_nt(message_grad, w_top[...])
        ).astype(BF16)

    loop(n_col, top_grad)

    def middle_pick(j):
        at = pl.ds(pl.multiple_of(j * bs, bs), bs)
        index = jnp.broadcast_to(middle_pool[pl.ds(j, 1), :].astype(F32), (bs, bs)).T
        maps = []
        for i in range(n_col):
            ids = (lax.broadcasted_iota(jnp.int32, (bs, bs), 1) + i * bs).astype(F32)
            maps.append(jnp.where(ids == index, 1.0, 0.0).astype(BF16))
        picked = mm(jnp.concatenate(maps, axis=1), t_table[...]) * p3
        table[at, :] = (m_hidden[at, :] + picked[:, :width]).astype(BF16)
        grad = m_gsum[at, :] + picked[:, width:]
        m_gsum[at, :] = grad
        m_grad[j] = (grad * m_slope[at, :]).astype(BF16)

    loop(m_blocks, middle_pick)

    def middle_back(t):
        chain[t + 1] = mm(bank_t[middle_kind[t]], m_grad[middle_target[t]]) + chain[prev[3, t]]

    m_count = middle_kind.shape[0]
    loop(m_count, middle_back, UNROLL)
    for k in range(2):
        for i in range(m_send_n):
            m_back[k, i] = chain[last[3, m_blocks + k * m_send_n + i]].astype(BF16)
    for item in m_homes:
        item.start()

    pair = 2
    wide = pair * bs

    def fine_pick(j):
        at = pl.ds(pl.multiple_of(j * wide, wide), wide)
        fine_out[at, :] = (hidden[at, :] + p2 * mm(pick_map[at, :], table[...])).astype(BF16)

    loop(rows // wide, fine_pick)
    weight_out[2] = mm_tn(top_h[...].reshape(t_rows, width), t_gmsg[...]) * t_rows ** (-0.5)
    for item in m_homes:
        item.wait()
    for k in range(2):
        for i in range(m_send_n):
            t = m_count + k * m_send_n + i
            chain[t + 1] = m_home[k, i].astype(F32) + chain[prev[3, t]]

    def middle_grad(b):
        at = pl.ds(pl.multiple_of(b * bs, bs), bs)
        message_grad = chain[last[3, b]].astype(BF16)
        m_gmsg[at, :] = message_grad
        table[at, :] = (m_gsum[at, :] + mm_nt(message_grad, w_middle[...])).astype(BF16)

    loop(m_blocks, middle_grad)
    mg_slots[r] = (mm_tn(m_low[...], m_gmsg[...]) * (m_rows * n_row) ** (-0.5)).astype(BF16)
    sum_middle.start()

    def fine_grad_pick(j):
        at = pl.ds(pl.multiple_of(j * wide, wide), wide)
        grad = cot[at, :].astype(F32) + p2 * mm(pick_map[at, :], table[...])
        grad_hidden[at, :] = grad
        grad = (grad * slope[at, :]).astype(BF16)
        grad_blocks[pl.ds(j * pair, pair)] = grad.reshape(pair, bs, width)

    loop(rows // wide, fine_grad_pick)

    f_count = fine_kind.shape[0]

    def fine_back(t):
        chain[t + 1] = mm(bank_t[fine_kind[t]], grad_blocks[fine_target[t]]) + chain[prev[1, t]]

    loop(f_count, fine_back, UNROLL)
    for k in range(4):
        for i in range(send):
            back_fine[k, i] = chain[last[1, blocks + k * send + i]].astype(BF16)
    for item in home:
        item.start()
    sum_middle.wait()
    weight_out[1] = sum_middle.total()
    for item in home:
        item.wait()
    for k in range(4):
        for i in range(send):
            t = f_count + k * send + i
            chain[t + 1] = home_fine[k, i].astype(F32) + chain[prev[1, t]]

    def fine_message_grad(b):
        at = pl.ds(pl.multiple_of(b * bs, bs), bs)
        grad_sum[at, :] = chain[last[1, b]].astype(BF16)

    loop(blocks, fine_message_grad)
    scale = (rows * n_row * n_col) ** (-0.5)
    fg_slots_col[c] = (mm_tn(feat[...], grad_sum[...]) * scale).astype(BF16)
    sum_fine_col.start()

    def fine_final(b):
        at = pl.ds(pl.multiple_of(b * bs, bs), bs)
        grad_out[at, :] = (grad_hidden[at, :] + mm_nt(grad_sum[at, :], w_fine[...])).astype(BF16)

    loop(blocks // 2, fine_final)
    sum_fine_col.wait()
    fg_slots_row[r] = sum_fine_col.total().astype(BF16)
    sum_fine_row.start()
    loop(blocks // 2, lambda b: fine_final(b + blocks // 2))
    sum_fine_row.wait()
    weight_out[0] = sum_fine_row.total()


def links(keys, live, extent):
    pos = jnp.arange(keys.shape[1], dtype=jnp.int32)
    valid = live[:, None, :]
    same = (keys[:, :, None] == keys[:, None, :]) & (pos[None, None, :] < pos[None, :, None]) & valid
    prev = jnp.max(jnp.where(same, pos + 1, 0), axis=2)
    ids = jnp.arange(extent, dtype=jnp.int32)
    ends = (keys[:, None, :] == ids[None, :, None]) & valid
    last = jnp.max(jnp.where(ends, pos + 1, 0), axis=2)
    return prev, last


def local(
    features,
    cotangent,
    fine_weight,
    middle_weight,
    top_weight,
    tile_bank,
    fine_source,
    fine_target,
    fine_kind,
    tile_count,
    fine_sends,
    fine_pool,
    middle_source,
    middle_target,
    middle_kind,
    middle_sends,
    middle_pool,
    top_source,
    top_kind,
):
    n_row = lax.axis_size("row")
    n_col = lax.axis_size("col")
    bs = tile_bank.shape[1]
    kinds = tile_bank.shape[0]
    rows, width = features.shape
    blocks = rows // bs
    send = fine_sends.shape[0] // 4
    m_rows = middle_pool.shape[0]
    m_blocks = m_rows // bs
    m_send = middle_sends.shape[0] // 2
    t_slots = top_source.shape[0] // n_col
    chunk = m_rows // n_col
    f_count = fine_kind.shape[0]
    length = f_count + 4 * send
    extent = max(blocks + 4 * send, m_blocks + 2 * m_send, n_col)

    def padded(*pieces):
        key = jnp.concatenate(pieces)
        return jnp.pad(key, (0, length - key.shape[0]), constant_values=-1)

    keys = jnp.stack(
        [
            padded(fine_target),
            padded(fine_source, fine_sends),
            padded(middle_target),
            padded(middle_source, middle_sends),
            padded(top_source),
        ]
    )
    pos = jnp.arange(length, dtype=jnp.int32)
    alive = (pos < tile_count[0]) | (pos >= f_count)
    level = jnp.arange(5, dtype=jnp.int32)
    live = alive[None, :] | (level[:, None] >= 2)
    prev, last = links(keys, live, extent)

    def block_buf(*lead):
        return pltpu.VMEM(lead + (bs, width), BF16)

    def wide_buf(count, dtype):
        return pltpu.VMEM((count, width), dtype)

    part = pltpu.VMEM((n_col, chunk, width), BF16)
    n_sem = 12 + 8 * n_col + 4 * n_row
    scratch = [
        block_buf(kinds),
        pltpu.VMEM((m_rows, rows), BF16),
        pltpu.VMEM((rows, m_rows), BF16),
        pltpu.VMEM((length + 1, bs, width), F32),
        block_buf(blocks + 4 * send),
        block_buf(4, send),
        block_buf(4, send),
        block_buf(4, send),
        wide_buf(rows, F32),
        wide_buf(rows, F32),
        wide_buf(rows, F32),
        wide_buf(rows, BF16),
        block_buf(blocks),
        part,
        part,
        part,
        part,
        part,
        part,
        block_buf(m_blocks + 2 * m_send),
        block_buf(2, m_send),
        block_buf(2, m_send),
        block_buf(2, m_send),
        wide_buf(m_rows, F32),
        wide_buf(m_rows, F32),
        block_buf(m_blocks),
        wide_buf(m_rows, BF16),
        wide_buf(m_rows, F32),
        wide_buf(m_rows, BF16),
        wide_buf(m_rows, BF16),
        block_buf(n_row),
        block_buf(n_row),
        block_buf(n_col),
        block_buf(n_col),
        block_buf(n_col),
        block_buf(n_col),
        pltpu.VMEM((8, width), F32),
        wide_buf(n_col * bs, BF16),
        pltpu.VMEM((n_col * bs, 2 * width), BF16),
        block_buf(n_row),
        block_buf(n_col),
        block_buf(n_row),
        pltpu.SemaphoreType.DMA((n_sem,)),
        pltpu.SemaphoreType.DMA((n_sem,)),
    ]
    smem = pl.BlockSpec(memory_space=pltpu.SMEM)
    vmem = pl.BlockSpec(memory_space=pltpu.VMEM)
    return pl.pallas_call(
        functools.partial(kernel, (n_row, n_col, send, m_send, t_slots)),
        out_shape=(
            jax.ShapeDtypeStruct((rows, width), BF16),
            jax.ShapeDtypeStruct((rows, width), BF16),
            jax.ShapeDtypeStruct((3, width, width), F32),
        ),
        in_specs=[smem] * 12 + [vmem] * 8,
        out_specs=(vmem, vmem, vmem),
        scratch_shapes=scratch,
        compiler_params=pltpu.CompilerParams(
            collective_id=0, has_side_effects=True, vmem_limit_bytes=48 * 1024 * 1024
        ),
        cost_estimate=pl.CostEstimate(
            flops=4_000_000_000, bytes_accessed=4_000_000, transcendentals=400_000
        ),
    )(
        prev,
        last,
        fine_source,
        fine_target,
        fine_kind,
        fine_sends,
        middle_source,
        middle_target,
        middle_kind,
        middle_sends,
        top_source,
        top_kind,
        features,
        cotangent,
        fine_weight,
        middle_weight,
        top_weight,
        tile_bank,
        fine_pool.reshape(blocks, bs),
        middle_pool.reshape(m_blocks, bs),
    )


def solution(mesh):
    everywhere = P(("group", "row", "col"))
    by_row = P(("group", "row"))
    in_specs = (
        (P(("group", "row", "col"), None),) * 2
        + (P(),) * 4
        + (everywhere,) * 6
        + (by_row,) * 5
        + (P("group"),) * 2
    )
    out_specs = (
        P(("group", "row", "col"), None),
        P(("group", "row", "col"), None),
        P("group", None, None),
    )
    return jax.shard_map(local, mesh=mesh, in_specs=in_specs, out_specs=out_specs, check_vma=False)
```

```python
import functools

import jax
import jax.numpy as jnp
from jax import lax
from jax.experimental import pallas as pl
from jax.experimental.pallas import tpu as pltpu
from jax.sharding import PartitionSpec as P

MESH = pl.DeviceIdType.MESH
F32 = jnp.float32
BF16 = jnp.bfloat16
UNROLL = 8


def gelu_pair(x):
    k = 0.7978845608028654
    a = 0.044715
    square = x * x
    t = jnp.tanh(k * (x + a * (square * x)))
    half = 0.5 + 0.5 * t
    slope = half + (0.5 * k) * x * ((1.0 - t * t) * (1.0 + (3.0 * a) * square))
    return x * half, slope


def mm(a, b):
    return jnp.dot(a, b, preferred_element_type=F32)


def mm_tn(a, b):
    return lax.dot_general(a, b, (((0,), (0,)), ((), ())), preferred_element_type=F32)


def mm_nt(a, b):
    return lax.dot_general(a, b, (((1,), (1,)), ((), ())), preferred_element_type=F32)


def loop(count, body, unroll=1):
    while count % unroll:
        unroll //= 2

    def step(index, carry):
        for inner in range(unroll):
            body(index * unroll + inner)
        return carry

    lax.fori_loop(0, count // unroll, step, 0)


def kernel(
    dims,
    tile_count,
    fine_source,
    fine_target,
    fine_kind,
    fine_sends,
    middle_source,
    middle_target,
    middle_kind,
    middle_sends,
    top_source,
    top_kind,
    *refs,
):
    n = 15
    inputs, results, held = refs[:n], refs[n : n + 3], refs[n + 3 : 2 * n + 3]
    run(dims, tile_count, fine_source, fine_target, fine_kind, fine_sends, middle_source,
        middle_target, middle_kind, middle_sends, top_source, top_kind, inputs, held,
        *held[:8], *results, *refs[2 * n + 3 :])


def run(
    dims,
    tile_count,
    fine_source,
    fine_target,
    fine_kind,
    fine_sends,
    middle_source,
    middle_target,
    middle_kind,
    middle_sends,
    top_source,
    top_kind,
    inputs,
    held,
    feat,
    cot,
    w_fine,
    w_middle,
    w_top,
    bank,
    fine_pool,
    middle_pool,
    fine_out,
    grad_out,
    weight_out,
    bank_t,
    pool_map,
    pick_map,
    chain,
    ext,
    send_fine,
    back_fine,
    home_fine,
    hidden,
    slope,
    grad_hidden,
    grad_sum,
    grad_blocks,
    part_h,
    part_g,
    slots_h,
    slots_g,
    full_h,
    full_g,
    m_ext,
    m_send,
    m_back,
    m_home,
    m_hidden,
    m_slope,
    m_grad,
    m_low,
    m_gsum,
    m_gmsg,
    table,
    top_slots_h,
    top_slots_g,
    top_h,
    top_g,
    t_msg,
    t_gsum,
    t_gmsg,
    t_table,
    mg_slots,
    fg_slots_col,
    fg_slots_row,
    top_map,
    middle_map,
    key_rows,
    link_rows,
    link,
    load_sem,
    send_sem,
    recv_sem,
):
    n_row, n_col, send, m_send_n, t_slots = dims
    r = lax.axis_index("row")
    c = lax.axis_index("col")
    place = {"row": (r, n_row), "col": (c, n_col)}
    kinds, bs, width = bank.shape
    rows = feat.shape[0]
    blocks = rows // bs
    m_rows = m_low.shape[0]
    m_blocks = m_rows // bs
    t_rows = n_col * bs
    chunk = m_rows // n_col
    p2 = (m_rows / (rows * n_col)) ** 0.5
    p3 = (t_rows / (m_rows * n_row)) ** 0.5
    allotted = [0]

    def semaphores(count):
        base = allotted[0]
        allotted[0] += count
        return base

    def remote(src, dst, s, v, axis, target):
        return pltpu.make_async_remote_copy(
            src_ref=src,
            dst_ref=dst,
            send_sem=send_sem.at[s],
            recv_sem=recv_sem.at[v],
            device_id={axis: target},
            device_id_type=MESH,
        )

    class Exchange:
        def __init__(self, source, slots, axis):
            self.source, self.slots, self.axis = source, slots, axis
            self.me, self.n = place[axis]
            self.base = semaphores(self.n)

        def peers(self):
            me, n = self.me, self.n
            if self.axis == "row" or n % 2:
                return [lax.rem(me + k, n) for k in range(1, n)]
            chip, core = me // 2, me % 2
            away = [
                lax.rem(chip + d, n // 2) * 2 + e for d in range(1, n // 2) for e in range(2)
            ]
            return away + [chip * 2 + 1 - core]

        def start(self, before=lambda p: None):
            for k, p in enumerate(self.peers()):
                before(p)
                remote(
                    self.source(p),
                    self.slots.at[self.me],
                    self.base + k,
                    self.base + self.me,
                    self.axis,
                    p,
                ).start()

        def wait(self):
            for k, p in enumerate(self.peers()):
                remote(
                    self.source(p),
                    self.slots.at[p],
                    self.base + k,
                    self.base + p,
                    self.axis,
                    p,
                ).wait()

        def total(self):
            value = self.slots[0].astype(F32)
            for k in range(1, self.n):
                value = value + self.slots[k].astype(F32)
            return value

    class Shift:
        def __init__(self, source, target, axis, delta):
            self.me, self.n = place[axis]
            self.base = semaphores(1)
            self.copy = lambda p: remote(source, target, self.base, self.base, axis, p)
            self.delta = delta
            low, high = self.me > 0, self.me < self.n - 1
            self.sends, self.gets = (high, low) if delta > 0 else (low, high)
            self.lacks = jnp.logical_not(self.gets)
            self.target = target

        def clear(self):
            @pl.when(self.lacks)
            def _():
                self.target[...] = jnp.zeros(self.target.shape, BF16)

        def start(self):
            @pl.when(self.sends)
            def _():
                self.copy(self.me + self.delta).start()

        def wait(self):
            other = jnp.clip(self.me + self.delta, 0, self.n - 1)

            @pl.when(self.sends)
            def _():
                self.copy(other).wait_send()

            @pl.when(self.gets)
            def _():
                self.copy(other).wait_recv()

    ways = (("row", 1), ("row", -1), ("col", 1), ("col", -1))
    halo = [
        Shift(send_fine.at[k], ext.at[pl.ds(blocks + send * k, send)], axis, delta)
        for k, (axis, delta) in enumerate(ways)
    ]
    home = [
        Shift(back_fine.at[k], home_fine.at[k], axis, -delta)
        for k, (axis, delta) in enumerate(ways)
    ]
    m_halo = [
        Shift(
            m_send.at[k], m_ext.at[pl.ds(m_blocks + m_send_n * k, m_send_n)], axis, delta
        )
        for k, (axis, delta) in enumerate(ways[:2])
    ]
    m_homes = [
        Shift(m_back.at[k], m_home.at[k], axis, -delta)
        for k, (axis, delta) in enumerate(ways[:2])
    ]
    scatter_h = Exchange(lambda p: part_h.at[p], slots_h, "col")
    scatter_g = Exchange(lambda p: part_g.at[p], slots_g, "col")
    gather_h = Exchange(lambda p: full_h.at[c], full_h, "col")
    gather_g = Exchange(lambda p: full_g.at[c], full_g, "col")
    rows_h = Exchange(lambda p: top_slots_h.at[r], top_slots_h, "row")
    rows_g = Exchange(lambda p: top_slots_g.at[r], top_slots_g, "row")
    cols_h = Exchange(lambda p: top_h.at[c], top_h, "col")
    cols_g = Exchange(lambda p: top_g.at[c], top_g, "col")
    sum_middle = Exchange(lambda p: mg_slots.at[r], mg_slots, "row")
    sum_fine_col = Exchange(lambda p: fg_slots_col.at[c], fg_slots_col, "col")
    sum_fine_row = Exchange(lambda p: fg_slots_row.at[r], fg_slots_row, "row")

    barrier = pltpu.get_barrier_semaphore()
    for axis in ("row", "col"):
        me, n = place[axis]
        for k in range(1, n):
            pl.semaphore_signal(
                barrier, inc=1, device_id={axis: lax.rem(me + k, n)}, device_id_type=MESH
            )
    loads = [
        pltpu.make_async_copy(src, dst, load_sem.at[k])
        for k, (src, dst) in enumerate(zip(inputs, held))
    ]
    order = [0, 2, 6, 1, 5, 7, 8, 9, 10, 11, 12, 13, 14, 3, 4]
    for k in order:
        loads[k].start()
    for item in halo + home + m_halo + m_homes:
        item.clear()
    chain[0] = jnp.zeros((bs, width), F32)

    def message(b):
        value = mm(feat[pl.ds(pl.multiple_of(b * bs, bs), bs), :], w_fine[...]).astype(BF16)
        ext[b] = value
        grad_blocks[b] = value

    loads[0].wait()
    loads[2].wait()
    loop(blocks, message, 4)
    for k in range(4):
        for i in range(send):
            send_fine[k, i] = grad_blocks[fine_sends[k * send + i]]
    pl.semaphore_wait(barrier, n_row + n_col - 2)
    for item in halo:
        item.start()

    for k in order[2:]:
        loads[k].wait()

    keys_f, keys_b, keys_bs, keys_m, keys_n, keys_ns, keys_t = held[8:]
    first = lax.broadcasted_iota(jnp.int32, (bs, bs), 0)
    second = lax.broadcasted_iota(jnp.int32, (bs, bs), 1)

    def spread(ref, line):
        key_rows[line : line + 1, : ref.shape[1]] = ref[...]
        across = jnp.broadcast_to(key_rows[line : line + 1, :], (bs, bs))
        return across, across.T

    def newest(found, offset):
        return jnp.max(jnp.where(found, first + (offset + 1), 0), axis=0, keepdims=True)

    key_rows[...] = jnp.full(key_rows.shape, -1, jnp.int32)

    def chain_of(line, main, live, more=None):
        count = main.shape[1]
        across, down = spread(main, 2 * line)
        valid = first < live
        prev_main = newest((across == down) & (first < second) & valid, 0)
        ends = newest((second == down) & valid, 0)
        if more is not None:
            across_more, down_more = spread(more, 2 * line + 1)
            known = first < more.shape[1]
            prev_more = jnp.maximum(
                newest((across_more == down) & valid, 0),
                newest((across_more == down_more) & (first < second) & known, count),
            )
            ends = jnp.maximum(ends, newest((second == down_more) & known, count))
            link_rows[3 * line + 1 : 3 * line + 2, :] = prev_more
        link_rows[3 * line : 3 * line + 1, :] = prev_main
        link_rows[3 * line + 2 : 3 * line + 3, :] = ends

    link_rows[...] = jnp.zeros(link_rows.shape, jnp.int32)
    chain_of(0, keys_f, tile_count[0])
    chain_of(1, keys_b, tile_count[0], keys_bs)
    chain_of(2, keys_m, keys_m.shape[1])
    chain_of(3, keys_n, keys_n.shape[1], keys_ns)
    chain_of(4, keys_t, keys_t.shape[1])
    link_copy = pltpu.make_async_copy(link_rows, link, load_sem.at[len(loads)])
    link_copy.start()

    def pool_block(j):
        index = fine_pool[pl.ds(j, 1), :]
        for i in range(m_blocks):
            ids = lax.broadcasted_iota(jnp.int32, (bs, bs), 0) + i * bs
            pool_map[i * bs : (i + 1) * bs, pl.ds(pl.multiple_of(j * bs, bs), bs)] = jnp.where(
                ids == index, 1.0, 0.0
            ).astype(BF16)

    loop(blocks, pool_block)

    def pooled(values, m):
        rows_at = pl.ds(pl.multiple_of(m * chunk, chunk), chunk)
        return mm(pool_map[rows_at, :], values[...]).astype(BF16)

    def pool_and_send(exchange, part, values):
        def one(p):
            part[p] = pooled(values, p)

        exchange.start(one)
        exchange.slots[c] = pooled(values, c)

    pool_and_send(scatter_g, part_g, cot)
    for j in range(m_blocks):
        ids = lax.broadcasted_iota(jnp.int32, (bs, bs), 0) + c * bs
        top_map[:, j * bs : (j + 1) * bs] = jnp.where(
            ids == middle_pool[j : j + 1, :], 1.0, 0.0
        ).astype(BF16)

    def flip(k):
        bank_t[k] = bank[k].astype(F32).T.astype(BF16)

    loop(kinds, flip, 4)
    for item in halo:
        item.wait()
    link_copy.wait()
    scatter_g.wait()
    full_g[c] = scatter_g.total().astype(BF16)
    gather_g.start()

    def fine_slot(t):
        chain[t + 1] = mm(bank[fine_kind[t]], ext[fine_source[t]]) + chain[link[0, t]]

    loop(fine_kind.shape[0], fine_slot, UNROLL)

    def fine_state(b):
        at = pl.ds(pl.multiple_of(b * bs, bs), bs)
        value, rate = gelu_pair(chain[link[2, b]])
        state = feat[at, :].astype(F32) + value
        hidden[at, :] = state
        slope[at, :] = rate
        grad_sum[at, :] = state.astype(BF16)

    loop(blocks, fine_state)
    pool_and_send(scatter_h, part_h, grad_sum)

    gather_g.wait()
    for k in range(n_col):
        m_gsum[k * chunk : (k + 1) * chunk, :] = full_g[k].astype(F32) * p2

    def top_partial(values):
        return mm(top_map[...], values)

    top_slots_g[r] = top_partial(m_gsum[...].astype(BF16)).astype(BF16)
    rows_g.start()

    def pick_block(j):
        index = jnp.broadcast_to(fine_pool[pl.ds(j, 1), :].astype(F32), (bs, bs)).T
        for i in range(m_blocks):
            ids = (lax.broadcasted_iota(jnp.int32, (bs, bs), 1) + i * bs).astype(F32)
            pick_map[pl.ds(pl.multiple_of(j * bs, bs), bs), i * bs : (i + 1) * bs] = jnp.where(
                ids == index, 1.0, 0.0
            ).astype(BF16)

    scatter_h.wait()
    full_h[c] = scatter_h.total().astype(BF16)
    gather_h.start()
    loop(blocks, pick_block)
    rows_g.wait()
    top_g[c] = (rows_g.total() * p3).astype(BF16)
    cols_g.start()
    gather_h.wait()

    for k in range(n_col):
        at = slice(k * chunk, (k + 1) * chunk)
        value = full_h[k].astype(F32) * p2
        m_hidden[at, :] = value
        m_low[at, :] = value.astype(BF16)
    for b in range(m_blocks):
        value = mm(m_low[b * bs : (b + 1) * bs, :], w_middle[...]).astype(BF16)
        m_ext[b] = value
        m_grad[b] = value
    for k in range(2):
        for i in range(m_send_n):
            m_send[k, i] = m_grad[middle_sends[k * m_send_n + i]]
    for item in m_halo:
        item.start()

    def middle_map_block(j):
        at = pl.ds(pl.multiple_of(j * bs, bs), bs)
        index = jnp.broadcast_to(middle_pool[pl.ds(j, 1), :].astype(F32), (bs, bs)).T
        for i in range(n_col):
            ids = (lax.broadcasted_iota(jnp.int32, (bs, bs), 1) + i * bs).astype(F32)
            middle_map[at, i * bs : (i + 1) * bs] = jnp.where(ids == index, 1.0, 0.0).astype(BF16)

    loop(m_blocks, middle_map_block)
    cols_g.wait()
    for item in m_halo:
        item.wait()

    def middle_slot(t):
        chain[t + 1] = mm(bank[middle_kind[t]], m_ext[middle_source[t]]) + chain[link[6, t]]

    loop(middle_kind.shape[0], middle_slot, UNROLL)

    def middle_state(b):
        at = pl.ds(pl.multiple_of(b * bs, bs), bs)
        value, rate = gelu_pair(chain[link[8, b]])
        m_hidden[at, :] = m_hidden[at, :] + value
        m_slope[at, :] = rate

    loop(m_blocks, middle_state)
    top_slots_h[r] = top_partial(m_hidden[...].astype(BF16)).astype(BF16)
    rows_h.start()
    rows_h.wait()
    top_h[c] = (rows_h.total() * p3).astype(BF16)
    cols_h.start()
    cols_h.wait()

    def top_message(b):
        t_msg[b] = mm(top_h[b], w_top[...]).astype(BF16)

    loop(n_col, top_message)

    def top_state(b):
        total = jnp.zeros((bs, width), F32)
        for s in range(t_slots):
            t = b * t_slots + s
            total = total + mm(bank[top_kind[t]], t_msg[top_source[t]])
        value, rate = gelu_pair(total)
        at = pl.ds(pl.multiple_of(b * bs, bs), bs)
        t_table[at, :width] = (top_h[b].astype(F32) + value).astype(BF16)
        t_gsum[b] = (top_g[b].astype(F32) * rate).astype(BF16)

    loop(n_col, top_state)

    def top_back(b):
        for s in range(t_slots):
            t = b * t_slots + s
            chain[t + 1] = mm(bank_t[top_kind[t]], t_gsum[b]) + chain[link[12, t]]

    loop(n_col, top_back)

    def top_grad(b):
        at = pl.ds(pl.multiple_of(b * bs, bs), bs)
        message_grad = chain[link[14, b]].astype(BF16)
        t_gmsg[at, :] = message_grad
        t_table[at, width:] = (
            top_g[b].astype(F32) + mm_nt(message_grad, w_top[...])
        ).astype(BF16)

    loop(n_col, top_grad)

    def middle_pick(j):
        at = pl.ds(pl.multiple_of(j * bs, bs), bs)
        picked = mm(middle_map[at, :], t_table[...]) * p3
        table[at, :] = (m_hidden[at, :] + picked[:, :width]).astype(BF16)
        grad = m_gsum[at, :] + picked[:, width:]
        m_gsum[at, :] = grad
        m_grad[j] = (grad * m_slope[at, :]).astype(BF16)

    loop(m_blocks, middle_pick)

    def middle_back(t):
        chain[t + 1] = mm(bank_t[middle_kind[t]], m_grad[middle_target[t]]) + chain[link[9, t]]

    m_count = middle_kind.shape[0]
    loop(m_count, middle_back, UNROLL)
    for k in range(2):
        for i in range(m_send_n):
            m_back[k, i] = chain[link[11, m_blocks + k * m_send_n + i]].astype(BF16)
    for item in m_homes:
        item.start()

    pair = 2
    wide = pair * bs

    def fine_pick(j):
        at = pl.ds(pl.multiple_of(j * wide, wide), wide)
        fine_out[at, :] = (hidden[at, :] + p2 * mm(pick_map[at, :], table[...])).astype(BF16)

    loop(rows // wide, fine_pick)
    weight_out[2] = mm_tn(top_h[...].reshape(t_rows, width), t_gmsg[...]) * t_rows ** (-0.5)
    for item in m_homes:
        item.wait()
    for k in range(2):
        for i in range(m_send_n):
            t = k * m_send_n + i
            chain[m_count + t + 1] = m_home[k, i].astype(F32) + chain[link[10, t]]

    def middle_grad(b):
        at = pl.ds(pl.multiple_of(b * bs, bs), bs)
        message_grad = chain[link[11, b]].astype(BF16)
        m_gmsg[at, :] = message_grad
        table[at, :] = (m_gsum[at, :] + mm_nt(message_grad, w_middle[...])).astype(BF16)

    loop(m_blocks, middle_grad)
    mg_slots[r] = (mm_tn(m_low[...], m_gmsg[...]) * (m_rows * n_row) ** (-0.5)).astype(BF16)
    sum_middle.start()

    def fine_grad_pick(j):
        at = pl.ds(pl.multiple_of(j * wide, wide), wide)
        grad = cot[at, :].astype(F32) + p2 * mm(pick_map[at, :], table[...])
        grad_hidden[at, :] = grad
        grad = (grad * slope[at, :]).astype(BF16)
        grad_blocks[pl.ds(j * pair, pair)] = grad.reshape(pair, bs, width)

    loop(rows // wide, fine_grad_pick)

    f_count = fine_kind.shape[0]

    def fine_back(t):
        chain[t + 1] = mm(bank_t[fine_kind[t]], grad_blocks[fine_target[t]]) + chain[link[3, t]]

    loop(f_count, fine_back, UNROLL)
    for k in range(4):
        for i in range(send):
            back_fine[k, i] = chain[link[5, blocks + k * send + i]].astype(BF16)
    for item in home:
        item.start()
    sum_middle.wait()
    weight_out[1] = sum_middle.total()
    for item in home:
        item.wait()
    for k in range(4):
        for i in range(send):
            t = k * send + i
            chain[f_count + t + 1] = home_fine[k, i].astype(F32) + chain[link[4, t]]

    def fine_message_grad(b):
        at = pl.ds(pl.multiple_of(b * bs, bs), bs)
        grad_sum[at, :] = chain[link[5, b]].astype(BF16)

    loop(blocks, fine_message_grad)
    scale = (rows * n_row * n_col) ** (-0.5)
    fg_slots_col[c] = (mm_tn(feat[...], grad_sum[...]) * scale).astype(BF16)
    sum_fine_col.start()

    def fine_final(b):
        at = pl.ds(pl.multiple_of(b * bs, bs), bs)
        grad_out[at, :] = (grad_hidden[at, :] + mm_nt(grad_sum[at, :], w_fine[...])).astype(BF16)

    loop(blocks // 2, fine_final)
    sum_fine_col.wait()
    fg_slots_row[r] = sum_fine_col.total().astype(BF16)
    sum_fine_row.start()
    loop(blocks // 2, lambda b: fine_final(b + blocks // 2))
    sum_fine_row.wait()
    weight_out[0] = sum_fine_row.total()


def local(
    features,
    cotangent,
    fine_weight,
    middle_weight,
    top_weight,
    tile_bank,
    fine_source,
    fine_target,
    fine_kind,
    tile_count,
    fine_sends,
    fine_pool,
    middle_source,
    middle_target,
    middle_kind,
    middle_sends,
    middle_pool,
    top_source,
    top_kind,
):
    n_row = lax.axis_size("row")
    n_col = lax.axis_size("col")
    bs = tile_bank.shape[1]
    kinds = tile_bank.shape[0]
    rows, width = features.shape
    blocks = rows // bs
    send = fine_sends.shape[0] // 4
    m_rows = middle_pool.shape[0]
    m_blocks = m_rows // bs
    m_send = middle_sends.shape[0] // 2
    t_slots = top_source.shape[0] // n_col
    chunk = m_rows // n_col
    f_count = fine_kind.shape[0]
    length = f_count + 4 * send
    def block_buf(*lead):
        return pltpu.VMEM(lead + (bs, width), BF16)

    def wide_buf(count, dtype):
        return pltpu.VMEM((count, width), dtype)

    part = pltpu.VMEM((n_col, chunk, width), BF16)
    n_sem = 12 + 8 * n_col + 4 * n_row
    arrays = [
        features,
        cotangent,
        fine_weight,
        middle_weight,
        top_weight,
        tile_bank,
        fine_pool.reshape(blocks, bs),
        middle_pool.reshape(m_blocks, bs),
    ] + [
        key.reshape(1, key.shape[0])
        for key in (
            fine_target,
            fine_source,
            fine_sends,
            middle_target,
            middle_source,
            middle_sends,
            top_source,
        )
    ]
    scratch = [pltpu.VMEM(array.shape, array.dtype) for array in arrays] + [
        block_buf(kinds),
        pltpu.VMEM((m_rows, rows), BF16),
        pltpu.VMEM((rows, m_rows), BF16),
        pltpu.VMEM((length + 1, bs, width), F32),
        block_buf(blocks + 4 * send),
        block_buf(4, send),
        block_buf(4, send),
        block_buf(4, send),
        wide_buf(rows, F32),
        wide_buf(rows, F32),
        wide_buf(rows, F32),
        wide_buf(rows, BF16),
        block_buf(blocks),
        part,
        part,
        part,
        part,
        part,
        part,
        block_buf(m_blocks + 2 * m_send),
        block_buf(2, m_send),
        block_buf(2, m_send),
        block_buf(2, m_send),
        wide_buf(m_rows, F32),
        wide_buf(m_rows, F32),
        block_buf(m_blocks),
        wide_buf(m_rows, BF16),
        wide_buf(m_rows, F32),
        wide_buf(m_rows, BF16),
        wide_buf(m_rows, BF16),
        block_buf(n_row),
        block_buf(n_row),
        block_buf(n_col),
        block_buf(n_col),
        block_buf(n_col),
        block_buf(n_col),
        wide_buf(n_col * bs, BF16),
        pltpu.VMEM((n_col * bs, 2 * width), BF16),
        block_buf(n_row),
        block_buf(n_col),
        block_buf(n_row),
        pltpu.VMEM((bs, m_rows), BF16),
        pltpu.VMEM((m_rows, n_col * bs), BF16),
        pltpu.VMEM((16, bs), jnp.int32),
        pltpu.VMEM((16, bs), jnp.int32),
        pltpu.SMEM((16, bs), jnp.int32),
        pltpu.SemaphoreType.DMA((len(arrays) + 1,)),
        pltpu.SemaphoreType.DMA((n_sem,)),
        pltpu.SemaphoreType.DMA((n_sem,)),
    ]
    smem = pl.BlockSpec(memory_space=pltpu.SMEM)
    vmem = pl.BlockSpec(memory_space=pltpu.VMEM)
    return pl.pallas_call(
        functools.partial(kernel, (n_row, n_col, send, m_send, t_slots)),
        out_shape=(
            jax.ShapeDtypeStruct((rows, width), BF16),
            jax.ShapeDtypeStruct((rows, width), BF16),
            jax.ShapeDtypeStruct((3, width, width), F32),
        ),
        in_specs=[smem] * 11 + [pl.BlockSpec(memory_space=pl.ANY)] * len(arrays),
        out_specs=(vmem, vmem, vmem),
        scratch_shapes=scratch,
        compiler_params=pltpu.CompilerParams(
            collective_id=0, has_side_effects=True, vmem_limit_bytes=56 * 1024 * 1024
        ),
        cost_estimate=pl.CostEstimate(
            flops=4_000_000_000, bytes_accessed=4_000_000, transcendentals=400_000
        ),
    )(
        tile_count,
        fine_source,
        fine_target,
        fine_kind,
        fine_sends,
        middle_source,
        middle_target,
        middle_kind,
        middle_sends,
        top_source,
        top_kind,
        *arrays,
    )


def solution(mesh):
    everywhere = P(("group", "row", "col"))
    by_row = P(("group", "row"))
    in_specs = (
        (P(("group", "row", "col"), None),) * 2
        + (P(),) * 4
        + (everywhere,) * 6
        + (by_row,) * 5
        + (P("group"),) * 2
    )
    out_specs = (
        P(("group", "row", "col"), None),
        P(("group", "row", "col"), None),
        P("group", None, None),
    )
    return jax.shard_map(local, mesh=mesh, in_specs=in_specs, out_specs=out_specs, check_vma=False)
```

```python
import functools

import jax
import jax.numpy as jnp
from jax import lax
from jax.experimental import pallas as pl
from jax.experimental.pallas import tpu as pltpu
from jax.sharding import PartitionSpec as P

MESH = pl.DeviceIdType.MESH
F32 = jnp.float32
BF16 = jnp.bfloat16
UNROLL = 8


def gelu_pair(x):
    k = 0.7978845608028654
    a = 0.044715
    square = x * x
    t = jnp.tanh(k * (x + a * (square * x)))
    half = 0.5 + 0.5 * t
    slope = half + (0.5 * k) * x * ((1.0 - t * t) * (1.0 + (3.0 * a) * square))
    return x * half, slope


def mm(a, b):
    return jnp.dot(a, b, preferred_element_type=F32)


def mm_tn(a, b):
    return lax.dot_general(a, b, (((0,), (0,)), ((), ())), preferred_element_type=F32)


def mm_nt(a, b):
    return lax.dot_general(a, b, (((1,), (1,)), ((), ())), preferred_element_type=F32)


def loop(count, body, unroll=1):
    while count % unroll:
        unroll //= 2

    def step(index, carry):
        for inner in range(unroll):
            body(index * unroll + inner)
        return carry

    lax.fori_loop(0, count // unroll, step, 0)


def kernel(
    dims,
    tile_count,
    fine_source,
    fine_target,
    fine_kind,
    fine_sends,
    middle_source,
    middle_target,
    middle_kind,
    middle_sends,
    top_source,
    top_kind,
    *refs,
):
    n = 15
    inputs, results, held = refs[:n], refs[n : n + 3], refs[n + 3 : 2 * n + 3]
    run(dims, tile_count, fine_source, fine_target, fine_kind, fine_sends, middle_source,
        middle_target, middle_kind, middle_sends, top_source, top_kind, inputs, held,
        *held[:8], *results, *refs[2 * n + 3 :])


def run(
    dims,
    tile_count,
    fine_source,
    fine_target,
    fine_kind,
    fine_sends,
    middle_source,
    middle_target,
    middle_kind,
    middle_sends,
    top_source,
    top_kind,
    inputs,
    held,
    feat,
    cot,
    w_fine,
    w_middle,
    w_top,
    bank,
    fine_pool,
    middle_pool,
    fine_out,
    grad_out,
    weight_out,
    bank_t,
    pool_map,
    pick_map,
    chain,
    ext,
    send_fine,
    back_fine,
    home_fine,
    hidden,
    slope,
    grad_hidden,
    grad_sum,
    grad_blocks,
    part_h,
    part_g,
    slots_h,
    slots_g,
    full_h,
    full_g,
    m_ext,
    m_send,
    m_back,
    m_home,
    m_hidden,
    m_slope,
    m_grad,
    m_low,
    m_gsum,
    m_gmsg,
    table,
    top_slots_h,
    top_slots_g,
    top_h,
    top_g,
    t_msg,
    t_gsum,
    t_gmsg,
    t_table,
    mg_slots,
    fg_slots_col,
    fg_slots_row,
    top_map,
    middle_map,
    key_rows,
    link_rows,
    link,
    load_sem,
    send_sem,
    recv_sem,
):
    n_row, n_col, send, m_send_n, t_slots = dims
    r = lax.axis_index("row")
    c = lax.axis_index("col")
    place = {"row": (r, n_row), "col": (c, n_col)}
    kinds, bs, width = bank.shape
    rows = feat.shape[0]
    blocks = rows // bs
    m_rows = m_low.shape[0]
    m_blocks = m_rows // bs
    t_rows = n_col * bs
    chunk = m_rows // n_col
    p2 = (m_rows / (rows * n_col)) ** 0.5
    p3 = (t_rows / (m_rows * n_row)) ** 0.5
    allotted = [0]

    def semaphores(count):
        base = allotted[0]
        allotted[0] += count
        return base

    def remote(src, dst, s, v, axis, target):
        return pltpu.make_async_remote_copy(
            src_ref=src,
            dst_ref=dst,
            send_sem=send_sem.at[s],
            recv_sem=recv_sem.at[v],
            device_id={axis: target},
            device_id_type=MESH,
        )

    class Exchange:
        def __init__(self, source, slots, axis):
            self.source, self.slots, self.axis = source, slots, axis
            self.me, self.n = place[axis]
            self.base = semaphores(self.n)

        def peers(self):
            me, n = self.me, self.n
            if self.axis == "row" or n % 2:
                return [lax.rem(me + k, n) for k in range(1, n)]
            chip, core = me // 2, me % 2
            away = [
                lax.rem(chip + d, n // 2) * 2 + e for d in range(1, n // 2) for e in range(2)
            ]
            return away + [chip * 2 + 1 - core]

        def start(self, before=lambda p: None):
            for k, p in enumerate(self.peers()):
                before(p)
                remote(
                    self.source(p),
                    self.slots.at[self.me],
                    self.base + k,
                    self.base + self.me,
                    self.axis,
                    p,
                ).start()

        def wait(self):
            for k, p in enumerate(self.peers()):
                remote(
                    self.source(p),
                    self.slots.at[p],
                    self.base + k,
                    self.base + p,
                    self.axis,
                    p,
                ).wait()

        def total(self):
            value = self.slots[0].astype(F32)
            for k in range(1, self.n):
                value = value + self.slots[k].astype(F32)
            return value

    class Shift:
        def __init__(self, source, target, axis, delta):
            self.me, self.n = place[axis]
            self.base = semaphores(1)
            self.copy = lambda p: remote(source, target, self.base, self.base, axis, p)
            self.delta = delta
            low, high = self.me > 0, self.me < self.n - 1
            self.sends, self.gets = (high, low) if delta > 0 else (low, high)
            self.lacks = jnp.logical_not(self.gets)
            self.target = target

        def clear(self):
            @pl.when(self.lacks)
            def _():
                self.target[...] = jnp.zeros(self.target.shape, BF16)

        def start(self):
            @pl.when(self.sends)
            def _():
                self.copy(self.me + self.delta).start()

        def wait(self):
            other = jnp.clip(self.me + self.delta, 0, self.n - 1)

            @pl.when(self.sends)
            def _():
                self.copy(other).wait_send()

            @pl.when(self.gets)
            def _():
                self.copy(other).wait_recv()

    ways = (("row", 1), ("row", -1), ("col", 1), ("col", -1))
    halo = [
        Shift(send_fine.at[k], ext.at[pl.ds(blocks + send * k, send)], axis, delta)
        for k, (axis, delta) in enumerate(ways)
    ]
    home = [
        Shift(back_fine.at[k], home_fine.at[k], axis, -delta)
        for k, (axis, delta) in enumerate(ways)
    ]
    m_halo = [
        Shift(
            m_send.at[k], m_ext.at[pl.ds(m_blocks + m_send_n * k, m_send_n)], axis, delta
        )
        for k, (axis, delta) in enumerate(ways[:2])
    ]
    m_homes = [
        Shift(m_back.at[k], m_home.at[k], axis, -delta)
        for k, (axis, delta) in enumerate(ways[:2])
    ]
    scatter_h = Exchange(lambda p: part_h.at[p], slots_h, "col")
    scatter_g = Exchange(lambda p: part_g.at[p], slots_g, "col")
    gather_h = Exchange(lambda p: full_h.at[c], full_h, "col")
    gather_g = Exchange(lambda p: full_g.at[c], full_g, "col")
    rows_h = Exchange(lambda p: top_slots_h.at[r], top_slots_h, "row")
    rows_g = Exchange(lambda p: top_slots_g.at[r], top_slots_g, "row")
    cols_h = Exchange(lambda p: top_h.at[c], top_h, "col")
    cols_g = Exchange(lambda p: top_g.at[c], top_g, "col")
    sum_middle = Exchange(lambda p: mg_slots.at[r], mg_slots, "row")
    sum_fine_col = Exchange(lambda p: fg_slots_col.at[c], fg_slots_col, "col")
    sum_fine_row = Exchange(lambda p: fg_slots_row.at[r], fg_slots_row, "row")

    barrier = pltpu.get_barrier_semaphore()
    for axis in ("row", "col"):
        me, n = place[axis]
        for k in range(1, n):
            pl.semaphore_signal(
                barrier, inc=1, device_id={axis: lax.rem(me + k, n)}, device_id_type=MESH
            )
    loads = [
        pltpu.make_async_copy(src, dst, load_sem.at[k])
        for k, (src, dst) in enumerate(zip(inputs, held))
    ]
    order = [0, 2, 6, 1, 5, 7, 8, 9, 10, 11, 12, 13, 14, 3, 4]
    for k in order:
        loads[k].start()
    for item in halo + home + m_halo + m_homes:
        item.clear()
    chain[0] = jnp.zeros((bs, width), F32)

    def message(b):
        value = mm(feat[pl.ds(pl.multiple_of(b * bs, bs), bs), :], w_fine[...]).astype(BF16)
        ext[b] = value
        grad_blocks[b] = value

    loads[0].wait()
    loads[2].wait()
    loop(blocks, message, 4)
    for k in range(4):
        for i in range(send):
            send_fine[k, i] = grad_blocks[fine_sends[k * send + i]]
    pl.semaphore_wait(barrier, n_row + n_col - 2)
    for item in halo:
        item.start()

    for k in order[2:]:
        loads[k].wait()

    keys_f, keys_b, keys_bs, keys_m, keys_n, keys_ns, keys_t = held[8:]
    first = lax.broadcasted_iota(jnp.int32, (bs, bs), 0)
    second = lax.broadcasted_iota(jnp.int32, (bs, bs), 1)

    def spread(ref, line):
        key_rows[line : line + 1, : ref.shape[1]] = ref[...]
        across = jnp.broadcast_to(key_rows[line : line + 1, :], (bs, bs))
        return across, across.T

    def newest(found, offset):
        return jnp.max(jnp.where(found, first + (offset + 1), 0), axis=0, keepdims=True)

    key_rows[...] = jnp.full(key_rows.shape, -1, jnp.int32)

    def chain_of(line, main, live, more=None):
        count = main.shape[1]
        across, down = spread(main, 2 * line)
        valid = first < live
        prev_main = newest((across == down) & (first < second) & valid, 0)
        ends = newest((second == down) & valid, 0)
        if more is not None:
            across_more, down_more = spread(more, 2 * line + 1)
            known = first < more.shape[1]
            prev_more = jnp.maximum(
                newest((across_more == down) & valid, 0),
                newest((across_more == down_more) & (first < second) & known, count),
            )
            ends = jnp.maximum(ends, newest((second == down_more) & known, count))
            link_rows[3 * line + 1 : 3 * line + 2, :] = prev_more
        link_rows[3 * line : 3 * line + 1, :] = prev_main
        link_rows[3 * line + 2 : 3 * line + 3, :] = ends

    link_rows[...] = jnp.zeros(link_rows.shape, jnp.int32)
    chain_of(0, keys_f, tile_count[0])
    chain_of(1, keys_b, tile_count[0], keys_bs)
    chain_of(2, keys_m, keys_m.shape[1])
    chain_of(3, keys_n, keys_n.shape[1], keys_ns)
    chain_of(4, keys_t, keys_t.shape[1])
    link_copy = pltpu.make_async_copy(link_rows, link, load_sem.at[len(loads)])
    link_copy.start()

    def pool_block(j):
        index = fine_pool[pl.ds(j, 1), :]
        for i in range(m_blocks):
            ids = lax.broadcasted_iota(jnp.int32, (bs, bs), 0) + i * bs
            pool_map[i * bs : (i + 1) * bs, pl.ds(pl.multiple_of(j * bs, bs), bs)] = jnp.where(
                ids == index, 1.0, 0.0
            ).astype(BF16)

    loop(blocks, pool_block)

    def pooled(values, m):
        rows_at = pl.ds(pl.multiple_of(m * chunk, chunk), chunk)
        return mm(pool_map[rows_at, :], values[...]).astype(BF16)

    def pool_and_send(exchange, part, values):
        def one(p):
            part[p] = pooled(values, p)

        exchange.start(one)
        exchange.slots[c] = pooled(values, c)

    pool_and_send(scatter_g, part_g, cot)
    for j in range(m_blocks):
        ids = lax.broadcasted_iota(jnp.int32, (bs, bs), 0) + c * bs
        top_map[:, j * bs : (j + 1) * bs] = jnp.where(
            ids == middle_pool[j : j + 1, :], 1.0, 0.0
        ).astype(BF16)

    for item in halo:
        item.wait()
    link_copy.wait()

    def fine_slot(t):
        chain[t + 1] = mm(bank[fine_kind[t]], ext[fine_source[t]]) + chain[link[0, t]]

    half = fine_kind.shape[0] // 2
    loop(half, fine_slot, UNROLL)
    scatter_g.wait()
    full_g[c] = scatter_g.total().astype(BF16)
    gather_g.start()
    loop(half, lambda t: fine_slot(t + half), UNROLL)

    def fine_state(b):
        at = pl.ds(pl.multiple_of(b * bs, bs), bs)
        total = chain[link[2, b]]
        state = feat[at, :].astype(F32) + gelu_pair(total)[0]
        hidden[at, :] = state
        slope[at, :] = total
        grad_sum[at, :] = state.astype(BF16)

    loop(blocks, fine_state)
    pool_and_send(scatter_h, part_h, grad_sum)

    gather_g.wait()
    for k in range(n_col):
        m_gsum[k * chunk : (k + 1) * chunk, :] = full_g[k].astype(F32) * p2

    def top_partial(values):
        return mm(top_map[...], values)

    top_slots_g[r] = top_partial(m_gsum[...].astype(BF16)).astype(BF16)
    rows_g.start()

    def pick_block(j):
        index = jnp.broadcast_to(fine_pool[pl.ds(j, 1), :].astype(F32), (bs, bs)).T
        for i in range(m_blocks):
            ids = (lax.broadcasted_iota(jnp.int32, (bs, bs), 1) + i * bs).astype(F32)
            pick_map[pl.ds(pl.multiple_of(j * bs, bs), bs), i * bs : (i + 1) * bs] = jnp.where(
                ids == index, 1.0, 0.0
            ).astype(BF16)

    scatter_h.wait()
    full_h[c] = scatter_h.total().astype(BF16)
    gather_h.start()
    loop(blocks, pick_block)
    rows_g.wait()
    top_g[c] = (rows_g.total() * p3).astype(BF16)
    cols_g.start()
    gather_h.wait()

    for k in range(n_col):
        at = slice(k * chunk, (k + 1) * chunk)
        value = full_h[k].astype(F32) * p2
        m_hidden[at, :] = value
        m_low[at, :] = value.astype(BF16)
    for b in range(m_blocks):
        value = mm(m_low[b * bs : (b + 1) * bs, :], w_middle[...]).astype(BF16)
        m_ext[b] = value
        m_grad[b] = value
    for k in range(2):
        for i in range(m_send_n):
            m_send[k, i] = m_grad[middle_sends[k * m_send_n + i]]
    for item in m_halo:
        item.start()

    def middle_map_block(j):
        at = pl.ds(pl.multiple_of(j * bs, bs), bs)
        index = jnp.broadcast_to(middle_pool[pl.ds(j, 1), :].astype(F32), (bs, bs)).T
        for i in range(n_col):
            ids = (lax.broadcasted_iota(jnp.int32, (bs, bs), 1) + i * bs).astype(F32)
            middle_map[at, i * bs : (i + 1) * bs] = jnp.where(ids == index, 1.0, 0.0).astype(BF16)

    loop(m_blocks, middle_map_block)
    cols_g.wait()
    for item in m_halo:
        item.wait()

    def middle_slot(t):
        chain[t + 1] = mm(bank[middle_kind[t]], m_ext[middle_source[t]]) + chain[link[6, t]]

    loop(middle_kind.shape[0], middle_slot, UNROLL)

    def middle_state(b):
        at = pl.ds(pl.multiple_of(b * bs, bs), bs)
        value, rate = gelu_pair(chain[link[8, b]])
        m_hidden[at, :] = m_hidden[at, :] + value
        m_slope[at, :] = rate

    loop(m_blocks, middle_state)
    top_slots_h[r] = top_partial(m_hidden[...].astype(BF16)).astype(BF16)
    rows_h.start()

    def flip(k):
        bank_t[k] = bank[k].astype(F32).T.astype(BF16)

    loop(kinds, flip, 4)
    rows_h.wait()
    top_h[c] = (rows_h.total() * p3).astype(BF16)
    cols_h.start()

    def fine_slope(b):
        at = pl.ds(pl.multiple_of(b * bs, bs), bs)
        slope[at, :] = gelu_pair(slope[at, :])[1]

    loop(blocks, fine_slope)
    cols_h.wait()

    def top_message(b):
        t_msg[b] = mm(top_h[b], w_top[...]).astype(BF16)

    loop(n_col, top_message)

    def top_state(b):
        total = jnp.zeros((bs, width), F32)
        for s in range(t_slots):
            t = b * t_slots + s
            total = total + mm(bank[top_kind[t]], t_msg[top_source[t]])
        value, rate = gelu_pair(total)
        at = pl.ds(pl.multiple_of(b * bs, bs), bs)
        t_table[at, :width] = (top_h[b].astype(F32) + value).astype(BF16)
        t_gsum[b] = (top_g[b].astype(F32) * rate).astype(BF16)

    loop(n_col, top_state)

    def top_back(b):
        for s in range(t_slots):
            t = b * t_slots + s
            chain[t + 1] = mm(bank_t[top_kind[t]], t_gsum[b]) + chain[link[12, t]]

    loop(n_col, top_back)

    def top_grad(b):
        at = pl.ds(pl.multiple_of(b * bs, bs), bs)
        message_grad = chain[link[14, b]].astype(BF16)
        t_gmsg[at, :] = message_grad
        t_table[at, width:] = (
            top_g[b].astype(F32) + mm_nt(message_grad, w_top[...])
        ).astype(BF16)

    loop(n_col, top_grad)

    def middle_pick(j):
        at = pl.ds(pl.multiple_of(j * bs, bs), bs)
        picked = mm(middle_map[at, :], t_table[...]) * p3
        table[at, :] = (m_hidden[at, :] + picked[:, :width]).astype(BF16)
        grad = m_gsum[at, :] + picked[:, width:]
        m_gsum[at, :] = grad
        m_grad[j] = (grad * m_slope[at, :]).astype(BF16)

    loop(m_blocks, middle_pick)

    def middle_back(t):
        chain[t + 1] = mm(bank_t[middle_kind[t]], m_grad[middle_target[t]]) + chain[link[9, t]]

    m_count = middle_kind.shape[0]
    loop(m_count, middle_back, UNROLL)
    for k in range(2):
        for i in range(m_send_n):
            m_back[k, i] = chain[link[11, m_blocks + k * m_send_n + i]].astype(BF16)
    for item in m_homes:
        item.start()

    pair = 2
    wide = pair * bs

    def fine_pick(j):
        at = pl.ds(pl.multiple_of(j * wide, wide), wide)
        fine_out[at, :] = (hidden[at, :] + p2 * mm(pick_map[at, :], table[...])).astype(BF16)

    loop(rows // wide, fine_pick)
    weight_out[2] = mm_tn(top_h[...].reshape(t_rows, width), t_gmsg[...]) * t_rows ** (-0.5)
    for item in m_homes:
        item.wait()
    for k in range(2):
        for i in range(m_send_n):
            t = k * m_send_n + i
            chain[m_count + t + 1] = m_home[k, i].astype(F32) + chain[link[10, t]]

    def middle_grad(b):
        at = pl.ds(pl.multiple_of(b * bs, bs), bs)
        message_grad = chain[link[11, b]].astype(BF16)
        m_gmsg[at, :] = message_grad
        table[at, :] = (m_gsum[at, :] + mm_nt(message_grad, w_middle[...])).astype(BF16)

    loop(m_blocks, middle_grad)
    mg_slots[r] = (mm_tn(m_low[...], m_gmsg[...]) * (m_rows * n_row) ** (-0.5)).astype(BF16)
    sum_middle.start()

    def fine_grad_pick(j):
        at = pl.ds(pl.multiple_of(j * wide, wide), wide)
        grad = cot[at, :].astype(F32) + p2 * mm(pick_map[at, :], table[...])
        grad_hidden[at, :] = grad
        grad = (grad * slope[at, :]).astype(BF16)
        grad_blocks[pl.ds(j * pair, pair)] = grad.reshape(pair, bs, width)

    loop(rows // wide, fine_grad_pick)

    f_count = fine_kind.shape[0]

    def fine_back(t):
        chain[t + 1] = mm(bank_t[fine_kind[t]], grad_blocks[fine_target[t]]) + chain[link[3, t]]

    loop(f_count, fine_back, UNROLL)
    for k in range(4):
        for i in range(send):
            back_fine[k, i] = chain[link[5, blocks + k * send + i]].astype(BF16)
    for item in home:
        item.start()
    sum_middle.wait()
    weight_out[1] = sum_middle.total()
    for item in home:
        item.wait()
    for k in range(4):
        for i in range(send):
            t = k * send + i
            chain[f_count + t + 1] = home_fine[k, i].astype(F32) + chain[link[4, t]]

    def fine_message_grad(b):
        at = pl.ds(pl.multiple_of(b * bs, bs), bs)
        grad_sum[at, :] = chain[link[5, b]].astype(BF16)

    loop(blocks, fine_message_grad)
    scale = (rows * n_row * n_col) ** (-0.5)
    fg_slots_col[c] = (mm_tn(feat[...], grad_sum[...]) * scale).astype(BF16)
    sum_fine_col.start()

    def fine_final(b):
        at = pl.ds(pl.multiple_of(b * bs, bs), bs)
        grad_out[at, :] = (grad_hidden[at, :] + mm_nt(grad_sum[at, :], w_fine[...])).astype(BF16)

    loop(blocks // 2, fine_final)
    sum_fine_col.wait()
    fg_slots_row[r] = sum_fine_col.total().astype(BF16)
    sum_fine_row.start()
    loop(blocks // 2, lambda b: fine_final(b + blocks // 2))
    sum_fine_row.wait()
    weight_out[0] = sum_fine_row.total()


def local(
    features,
    cotangent,
    fine_weight,
    middle_weight,
    top_weight,
    tile_bank,
    fine_source,
    fine_target,
    fine_kind,
    tile_count,
    fine_sends,
    fine_pool,
    middle_source,
    middle_target,
    middle_kind,
    middle_sends,
    middle_pool,
    top_source,
    top_kind,
):
    n_row = lax.axis_size("row")
    n_col = lax.axis_size("col")
    bs = tile_bank.shape[1]
    kinds = tile_bank.shape[0]
    rows, width = features.shape
    blocks = rows // bs
    send = fine_sends.shape[0] // 4
    m_rows = middle_pool.shape[0]
    m_blocks = m_rows // bs
    m_send = middle_sends.shape[0] // 2
    t_slots = top_source.shape[0] // n_col
    chunk = m_rows // n_col
    f_count = fine_kind.shape[0]
    length = f_count + 4 * send
    def block_buf(*lead):
        return pltpu.VMEM(lead + (bs, width), BF16)

    def wide_buf(count, dtype):
        return pltpu.VMEM((count, width), dtype)

    part = pltpu.VMEM((n_col, chunk, width), BF16)
    n_sem = 12 + 8 * n_col + 4 * n_row
    arrays = [
        features,
        cotangent,
        fine_weight,
        middle_weight,
        top_weight,
        tile_bank,
        fine_pool.reshape(blocks, bs),
        middle_pool.reshape(m_blocks, bs),
    ] + [
        key.reshape(1, key.shape[0])
        for key in (
            fine_target,
            fine_source,
            fine_sends,
            middle_target,
            middle_source,
            middle_sends,
            top_source,
        )
    ]
    scratch = [pltpu.VMEM(array.shape, array.dtype) for array in arrays] + [
        block_buf(kinds),
        pltpu.VMEM((m_rows, rows), BF16),
        pltpu.VMEM((rows, m_rows), BF16),
        pltpu.VMEM((length + 1, bs, width), F32),
        block_buf(blocks + 4 * send),
        block_buf(4, send),
        block_buf(4, send),
        block_buf(4, send),
        wide_buf(rows, F32),
        wide_buf(rows, F32),
        wide_buf(rows, F32),
        wide_buf(rows, BF16),
        block_buf(blocks),
        part,
        part,
        part,
        part,
        part,
        part,
        block_buf(m_blocks + 2 * m_send),
        block_buf(2, m_send),
        block_buf(2, m_send),
        block_buf(2, m_send),
        wide_buf(m_rows, F32),
        wide_buf(m_rows, F32),
        block_buf(m_blocks),
        wide_buf(m_rows, BF16),
        wide_buf(m_rows, F32),
        wide_buf(m_rows, BF16),
        wide_buf(m_rows, BF16),
        block_buf(n_row),
        block_buf(n_row),
        block_buf(n_col),
        block_buf(n_col),
        block_buf(n_col),
        block_buf(n_col),
        wide_buf(n_col * bs, BF16),
        pltpu.VMEM((n_col * bs, 2 * width), BF16),
        block_buf(n_row),
        block_buf(n_col),
        block_buf(n_row),
        pltpu.VMEM((bs, m_rows), BF16),
        pltpu.VMEM((m_rows, n_col * bs), BF16),
        pltpu.VMEM((16, bs), jnp.int32),
        pltpu.VMEM((16, bs), jnp.int32),
        pltpu.SMEM((16, bs), jnp.int32),
        pltpu.SemaphoreType.DMA((len(arrays) + 1,)),
        pltpu.SemaphoreType.DMA((n_sem,)),
        pltpu.SemaphoreType.DMA((n_sem,)),
    ]
    smem = pl.BlockSpec(memory_space=pltpu.SMEM)
    vmem = pl.BlockSpec(memory_space=pltpu.VMEM)
    return pl.pallas_call(
        functools.partial(kernel, (n_row, n_col, send, m_send, t_slots)),
        out_shape=(
            jax.ShapeDtypeStruct((rows, width), BF16),
            jax.ShapeDtypeStruct((rows, width), BF16),
            jax.ShapeDtypeStruct((3, width, width), F32),
        ),
        in_specs=[smem] * 11 + [pl.BlockSpec(memory_space=pl.ANY)] * len(arrays),
        out_specs=(vmem, vmem, vmem),
        scratch_shapes=scratch,
        compiler_params=pltpu.CompilerParams(
            collective_id=0, has_side_effects=True, vmem_limit_bytes=48 * 1024 * 1024
        ),
        cost_estimate=pl.CostEstimate(
            flops=4_000_000_000, bytes_accessed=4_000_000, transcendentals=400_000
        ),
    )(
        tile_count,
        fine_source,
        fine_target,
        fine_kind,
        fine_sends,
        middle_source,
        middle_target,
        middle_kind,
        middle_sends,
        top_source,
        top_kind,
        *arrays,
    )


def solution(mesh):
    everywhere = P(("group", "row", "col"))
    by_row = P(("group", "row"))
    in_specs = (
        (P(("group", "row", "col"), None),) * 2
        + (P(),) * 4
        + (everywhere,) * 6
        + (by_row,) * 5
        + (P("group"),) * 2
    )
    out_specs = (
        P(("group", "row", "col"), None),
        P(("group", "row", "col"), None),
        P("group", None, None),
    )
    return jax.shard_map(local, mesh=mesh, in_specs=in_specs, out_specs=out_specs, check_vma=False)
```

```python
import functools

import jax
import jax.numpy as jnp
from jax import lax
from jax.experimental import pallas as pl
from jax.experimental.pallas import tpu as pltpu
from jax.sharding import PartitionSpec as P

MESH = pl.DeviceIdType.MESH
F32 = jnp.float32
BF16 = jnp.bfloat16
UNROLL = 8


def gelu_pair(x):
    k = 0.7978845608028654
    a = 0.044715
    square = x * x
    t = jnp.tanh(k * (x + a * (square * x)))
    half = 0.5 + 0.5 * t
    slope = half + (0.5 * k) * x * ((1.0 - t * t) * (1.0 + (3.0 * a) * square))
    return x * half, slope


def mm(a, b):
    return jnp.dot(a, b, preferred_element_type=F32)


def mm_tn(a, b):
    return lax.dot_general(a, b, (((0,), (0,)), ((), ())), preferred_element_type=F32)


def mm_nt(a, b):
    return lax.dot_general(a, b, (((1,), (1,)), ((), ())), preferred_element_type=F32)


def loop(count, body, unroll=1):
    while count % unroll:
        unroll //= 2

    def step(index, carry):
        for inner in range(unroll):
            body(index * unroll + inner)
        return carry

    lax.fori_loop(0, count // unroll, step, 0)


def kernel(
    dims,
    tile_count,
    fine_source,
    fine_target,
    fine_kind,
    fine_sends,
    middle_source,
    middle_target,
    middle_kind,
    middle_sends,
    top_source,
    top_kind,
    *refs,
):
    n = 15
    inputs, results, held = refs[:n], refs[n : n + 3], refs[n + 3 : 2 * n + 3]
    run(dims, tile_count, fine_source, fine_target, fine_kind, fine_sends, middle_source,
        middle_target, middle_kind, middle_sends, top_source, top_kind, inputs, held,
        *held[:8], *results, *refs[2 * n + 3 :])


def run(
    dims,
    tile_count,
    fine_source,
    fine_target,
    fine_kind,
    fine_sends,
    middle_source,
    middle_target,
    middle_kind,
    middle_sends,
    top_source,
    top_kind,
    inputs,
    held,
    feat,
    cot,
    w_fine,
    w_middle,
    w_top,
    bank,
    fine_pool,
    middle_pool,
    fine_out,
    grad_out,
    weight_out,
    bank_t,
    pool_map,
    pick_map,
    chain,
    ext,
    send_fine,
    back_fine,
    home_fine,
    hidden,
    slope,
    grad_hidden,
    grad_sum,
    grad_blocks,
    part_h,
    part_g,
    slots_h,
    slots_g,
    full_h,
    full_g,
    m_ext,
    m_send,
    m_back,
    m_home,
    m_hidden,
    m_slope,
    m_grad,
    m_low,
    m_gsum,
    m_gmsg,
    table,
    top_slots_h,
    top_slots_g,
    top_h,
    top_g,
    t_msg,
    t_gsum,
    t_gmsg,
    t_table,
    mg_slots,
    fg_slots_col,
    fg_slots_row,
    top_map,
    middle_map,
    key_rows,
    link_rows,
    link,
    load_sem,
    send_sem,
    recv_sem,
):
    n_row, n_col, send, m_send_n, t_slots = dims
    r = lax.axis_index("row")
    c = lax.axis_index("col")
    place = {"row": (r, n_row), "col": (c, n_col)}
    kinds, bs, width = bank.shape
    rows = feat.shape[0]
    blocks = rows // bs
    m_rows = m_low.shape[0]
    m_blocks = m_rows // bs
    t_rows = n_col * bs
    chunk = m_rows // n_col
    p2 = (m_rows / (rows * n_col)) ** 0.5
    p3 = (t_rows / (m_rows * n_row)) ** 0.5
    allotted = [0]

    def semaphores(count):
        base = allotted[0]
        allotted[0] += count
        return base

    def remote(src, dst, s, v, axis, target):
        return pltpu.make_async_remote_copy(
            src_ref=src,
            dst_ref=dst,
            send_sem=send_sem.at[s],
            recv_sem=recv_sem.at[v],
            device_id={axis: target},
            device_id_type=MESH,
        )

    class Exchange:
        def __init__(self, source, slots, axis):
            self.source, self.slots, self.axis = source, slots, axis
            self.me, self.n = place[axis]
            self.base = semaphores(self.n)

        def peers(self):
            me, n = self.me, self.n
            if self.axis == "row" or n % 2:
                return [lax.rem(me + k, n) for k in range(1, n)]
            chip, core = me // 2, me % 2
            away = [
                lax.rem(chip + d, n // 2) * 2 + e for d in range(1, n // 2) for e in range(2)
            ]
            return away + [chip * 2 + 1 - core]

        def start(self, before=lambda p: None):
            for k, p in enumerate(self.peers()):
                before(p)
                remote(
                    self.source(p),
                    self.slots.at[self.me],
                    self.base + k,
                    self.base + self.me,
                    self.axis,
                    p,
                ).start()

        def wait(self):
            for k, p in enumerate(self.peers()):
                remote(
                    self.source(p),
                    self.slots.at[p],
                    self.base + k,
                    self.base + p,
                    self.axis,
                    p,
                ).wait()

        def total(self):
            value = self.slots[0].astype(F32)
            for k in range(1, self.n):
                value = value + self.slots[k].astype(F32)
            return value

    class Shift:
        def __init__(self, source, target, axis, delta):
            self.me, self.n = place[axis]
            self.base = semaphores(1)
            self.copy = lambda p: remote(source, target, self.base, self.base, axis, p)
            self.delta = delta
            low, high = self.me > 0, self.me < self.n - 1
            self.sends, self.gets = (high, low) if delta > 0 else (low, high)
            self.lacks = jnp.logical_not(self.gets)
            self.target = target

        def clear(self):
            @pl.when(self.lacks)
            def _():
                self.target[...] = jnp.zeros(self.target.shape, BF16)

        def start(self):
            @pl.when(self.sends)
            def _():
                self.copy(self.me + self.delta).start()

        def wait(self):
            other = jnp.clip(self.me + self.delta, 0, self.n - 1)

            @pl.when(self.sends)
            def _():
                self.copy(other).wait_send()

            @pl.when(self.gets)
            def _():
                self.copy(other).wait_recv()

    ways = (("row", 1), ("row", -1), ("col", 1), ("col", -1))
    halo = [
        Shift(send_fine.at[k], ext.at[pl.ds(blocks + send * k, send)], axis, delta)
        for k, (axis, delta) in enumerate(ways)
    ]
    home = [
        Shift(back_fine.at[k], home_fine.at[k], axis, -delta)
        for k, (axis, delta) in enumerate(ways)
    ]
    m_halo = [
        Shift(
            m_send.at[k], m_ext.at[pl.ds(m_blocks + m_send_n * k, m_send_n)], axis, delta
        )
        for k, (axis, delta) in enumerate(ways[:2])
    ]
    m_homes = [
        Shift(m_back.at[k], m_home.at[k], axis, -delta)
        for k, (axis, delta) in enumerate(ways[:2])
    ]
    scatter_h = Exchange(lambda p: part_h.at[p], slots_h, "col")
    scatter_g = Exchange(lambda p: part_g.at[p], slots_g, "col")
    gather_h = Exchange(lambda p: full_h.at[c], full_h, "col")
    gather_g = Exchange(lambda p: full_g.at[c], full_g, "col")
    rows_h = Exchange(lambda p: top_slots_h.at[r], top_slots_h, "row")
    rows_g = Exchange(lambda p: top_slots_g.at[r], top_slots_g, "row")
    cols_h = Exchange(lambda p: top_h.at[c], top_h, "col")
    cols_g = Exchange(lambda p: top_g.at[c], top_g, "col")
    sum_middle = Exchange(lambda p: mg_slots.at[r], mg_slots, "row")
    sum_fine_col = Exchange(lambda p: fg_slots_col.at[c], fg_slots_col, "col")
    sum_fine_row = Exchange(lambda p: fg_slots_row.at[r], fg_slots_row, "row")

    barrier = pltpu.get_barrier_semaphore()
    for axis in ("row", "col"):
        me, n = place[axis]
        for k in range(1, n):
            pl.semaphore_signal(
                barrier, inc=1, device_id={axis: lax.rem(me + k, n)}, device_id_type=MESH
            )
    loads = [
        pltpu.make_async_copy(src, dst, load_sem.at[k])
        for k, (src, dst) in enumerate(zip(inputs, held))
    ]
    order = [0, 2, 6, 1, 5, 7, 8, 9, 10, 11, 12, 13, 14, 3, 4]
    for k in order:
        loads[k].start()
    for item in halo + home + m_halo + m_homes:
        item.clear()
    chain[0] = jnp.zeros((bs, width), F32)

    def message(b):
        value = mm(feat[pl.ds(pl.multiple_of(b * bs, bs), bs), :], w_fine[...]).astype(BF16)
        ext[b] = value
        grad_blocks[b] = value

    loads[0].wait()
    loads[2].wait()
    loop(blocks, message, 4)
    for k in range(4):
        for i in range(send):
            send_fine[k, i] = grad_blocks[fine_sends[k * send + i]]
    pl.semaphore_wait(barrier, n_row + n_col - 2)
    for item in halo:
        item.start()

    for k in order[2:]:
        loads[k].wait()

    keys_f, keys_b, keys_bs, keys_m, keys_n, keys_ns, keys_t = held[8:]
    first = lax.broadcasted_iota(jnp.int32, (bs, bs), 0)
    second = lax.broadcasted_iota(jnp.int32, (bs, bs), 1)

    def spread(ref, line):
        key_rows[line : line + 1, : ref.shape[1]] = ref[...]
        across = jnp.broadcast_to(key_rows[line : line + 1, :], (bs, bs))
        return across, across.T

    def newest(found, offset):
        return jnp.max(jnp.where(found, first + (offset + 1), 0), axis=0, keepdims=True)

    key_rows[...] = jnp.full(key_rows.shape, -1, jnp.int32)

    def chain_of(line, main, live, more=None):
        count = main.shape[1]
        across, down = spread(main, 2 * line)
        valid = first < live
        prev_main = newest((across == down) & (first < second) & valid, 0)
        ends = newest((second == down) & valid, 0)
        if more is not None:
            across_more, down_more = spread(more, 2 * line + 1)
            known = first < more.shape[1]
            prev_more = jnp.maximum(
                newest((across_more == down) & valid, 0),
                newest((across_more == down_more) & (first < second) & known, count),
            )
            ends = jnp.maximum(ends, newest((second == down_more) & known, count))
            link_rows[3 * line + 1 : 3 * line + 2, :] = prev_more
        link_rows[3 * line : 3 * line + 1, :] = prev_main
        link_rows[3 * line + 2 : 3 * line + 3, :] = ends

    link_rows[...] = jnp.zeros(link_rows.shape, jnp.int32)
    chain_of(0, keys_f, tile_count[0])
    chain_of(1, keys_b, tile_count[0], keys_bs)
    chain_of(2, keys_m, keys_m.shape[1])
    chain_of(3, keys_n, keys_n.shape[1], keys_ns)
    chain_of(4, keys_t, keys_t.shape[1])
    link_copy = pltpu.make_async_copy(link_rows, link, load_sem.at[len(loads)])
    link_copy.start()

    def pool_block(j):
        index = fine_pool[pl.ds(j, 1), :]
        for i in range(m_blocks):
            ids = lax.broadcasted_iota(jnp.int32, (bs, bs), 0) + i * bs
            pool_map[i * bs : (i + 1) * bs, pl.ds(pl.multiple_of(j * bs, bs), bs)] = jnp.where(
                ids == index, 1.0, 0.0
            ).astype(BF16)

    loop(blocks, pool_block)

    def pooled(values, m):
        rows_at = pl.ds(pl.multiple_of(m * chunk, chunk), chunk)
        return mm(pool_map[rows_at, :], values[...]).astype(BF16)

    def pool_and_send(exchange, part, values):
        def one(p):
            part[p] = pooled(values, p)

        exchange.start(one)
        exchange.slots[c] = pooled(values, c)

    pool_and_send(scatter_g, part_g, cot)
    for j in range(m_blocks):
        ids = lax.broadcasted_iota(jnp.int32, (bs, bs), 0) + c * bs
        top_map[:, j * bs : (j + 1) * bs] = jnp.where(
            ids == middle_pool[j : j + 1, :], 1.0, 0.0
        ).astype(BF16)

    for item in halo:
        item.wait()
    link_copy.wait()

    def fine_slot(t):
        chain[t + 1] = mm(bank[fine_kind[t]], ext[fine_source[t]]) + chain[link[0, t]]

    half = fine_kind.shape[0] // 2
    loop(half, fine_slot, UNROLL)
    scatter_g.wait()
    full_g[c] = scatter_g.total().astype(BF16)
    gather_g.start()
    loop(half, lambda t: fine_slot(t + half), UNROLL)

    def fine_state(b):
        at = pl.ds(pl.multiple_of(b * bs, bs), bs)
        total = chain[link[2, b]]
        state = feat[at, :].astype(F32) + gelu_pair(total)[0]
        hidden[at, :] = state
        slope[at, :] = total
        grad_sum[at, :] = state.astype(BF16)

    loop(blocks, fine_state)
    pool_and_send(scatter_h, part_h, grad_sum)

    gather_g.wait()
    for k in range(n_col):
        m_gsum[k * chunk : (k + 1) * chunk, :] = full_g[k].astype(F32) * p2

    def top_partial(values):
        return mm(top_map[...], values)

    top_slots_g[r] = top_partial(m_gsum[...].astype(BF16)).astype(BF16)
    rows_g.start()

    def pick_block(j):
        index = jnp.broadcast_to(fine_pool[pl.ds(j, 1), :].astype(F32), (bs, bs)).T
        for i in range(m_blocks):
            ids = (lax.broadcasted_iota(jnp.int32, (bs, bs), 1) + i * bs).astype(F32)
            pick_map[pl.ds(pl.multiple_of(j * bs, bs), bs), i * bs : (i + 1) * bs] = jnp.where(
                ids == index, 1.0, 0.0
            ).astype(BF16)

    scatter_h.wait()
    full_h[c] = scatter_h.total().astype(BF16)
    gather_h.start()
    loop(blocks, pick_block)
    rows_g.wait()
    top_g[c] = (rows_g.total() * p3).astype(BF16)
    cols_g.start()
    gather_h.wait()

    for k in range(n_col):
        at = slice(k * chunk, (k + 1) * chunk)
        value = full_h[k].astype(F32) * p2
        m_hidden[at, :] = value
        m_low[at, :] = value.astype(BF16)
    for b in range(m_blocks):
        value = mm(m_low[b * bs : (b + 1) * bs, :], w_middle[...]).astype(BF16)
        m_ext[b] = value
        m_grad[b] = value
    for k in range(2):
        for i in range(m_send_n):
            m_send[k, i] = m_grad[middle_sends[k * m_send_n + i]]
    for item in m_halo:
        item.start()

    def middle_map_block(j):
        at = pl.ds(pl.multiple_of(j * bs, bs), bs)
        index = jnp.broadcast_to(middle_pool[pl.ds(j, 1), :].astype(F32), (bs, bs)).T
        for i in range(n_col):
            ids = (lax.broadcasted_iota(jnp.int32, (bs, bs), 1) + i * bs).astype(F32)
            middle_map[at, i * bs : (i + 1) * bs] = jnp.where(ids == index, 1.0, 0.0).astype(BF16)

    loop(m_blocks, middle_map_block)
    cols_g.wait()
    for item in m_halo:
        item.wait()

    def middle_slot(t):
        chain[t + 1] = mm(bank[middle_kind[t]], m_ext[middle_source[t]]) + chain[link[6, t]]

    loop(middle_kind.shape[0], middle_slot, UNROLL)

    def middle_state(b):
        at = pl.ds(pl.multiple_of(b * bs, bs), bs)
        value, rate = gelu_pair(chain[link[8, b]])
        m_hidden[at, :] = m_hidden[at, :] + value
        m_slope[at, :] = rate

    loop(m_blocks, middle_state)
    top_slots_h[r] = top_partial(m_hidden[...].astype(BF16)).astype(BF16)
    rows_h.start()

    def flip(k):
        bank_t[k] = bank[k].astype(F32).T.astype(BF16)

    loop(kinds, flip, 4)
    rows_h.wait()
    top_h[c] = (rows_h.total() * p3).astype(BF16)
    cols_h.start()

    def fine_slope(b):
        at = pl.ds(pl.multiple_of(b * bs, bs), bs)
        slope[at, :] = gelu_pair(slope[at, :])[1]

    loop(blocks, fine_slope)
    cols_h.wait()

    def top_message(b):
        t_msg[b] = mm(top_h[b], w_top[...]).astype(BF16)

    loop(n_col, top_message)

    def top_state(b):
        total = jnp.zeros((bs, width), F32)
        for s in range(t_slots):
            t = b * t_slots + s
            total = total + mm(bank[top_kind[t]], t_msg[top_source[t]])
        value, rate = gelu_pair(total)
        at = pl.ds(pl.multiple_of(b * bs, bs), bs)
        t_table[at, :width] = (top_h[b].astype(F32) + value).astype(BF16)
        t_gsum[b] = (top_g[b].astype(F32) * rate).astype(BF16)

    loop(n_col, top_state)

    def top_back(b):
        for s in range(t_slots):
            t = b * t_slots + s
            chain[t + 1] = mm(bank_t[top_kind[t]], t_gsum[b]) + chain[link[12, t]]

    loop(n_col, top_back)

    def top_grad(b):
        at = pl.ds(pl.multiple_of(b * bs, bs), bs)
        message_grad = chain[link[14, b]].astype(BF16)
        t_gmsg[at, :] = message_grad
        t_table[at, width:] = (
            top_g[b].astype(F32) + mm_nt(message_grad, w_top[...])
        ).astype(BF16)

    loop(n_col, top_grad)

    def middle_pick(j):
        at = pl.ds(pl.multiple_of(j * bs, bs), bs)
        picked = mm(middle_map[at, :], t_table[...]) * p3
        table[at, :] = (m_hidden[at, :] + picked[:, :width]).astype(BF16)
        grad = m_gsum[at, :] + picked[:, width:]
        m_gsum[at, :] = grad
        m_grad[j] = (grad * m_slope[at, :]).astype(BF16)

    loop(m_blocks, middle_pick)

    def middle_back(t):
        chain[t + 1] = mm(bank_t[middle_kind[t]], m_grad[middle_target[t]]) + chain[link[9, t]]

    m_count = middle_kind.shape[0]
    loop(m_count, middle_back, UNROLL)
    for k in range(2):
        for i in range(m_send_n):
            m_back[k, i] = chain[link[11, m_blocks + k * m_send_n + i]].astype(BF16)
    for item in m_homes:
        item.start()

    pair = 2
    wide = pair * bs

    def fine_pick(j):
        at = pl.ds(pl.multiple_of(j * wide, wide), wide)
        fine_out[at, :] = (hidden[at, :] + p2 * mm(pick_map[at, :], table[...])).astype(BF16)

    loop(rows // wide, fine_pick)
    weight_out[2] = mm_tn(top_h[...].reshape(t_rows, width), t_gmsg[...]) * t_rows ** (-0.5)
    for item in m_homes:
        item.wait()
    for k in range(2):
        for i in range(m_send_n):
            t = k * m_send_n + i
            chain[m_count + t + 1] = m_home[k, i].astype(F32) + chain[link[10, t]]

    def middle_grad(b):
        at = pl.ds(pl.multiple_of(b * bs, bs), bs)
        message_grad = chain[link[11, b]].astype(BF16)
        m_gmsg[at, :] = message_grad
        table[at, :] = (m_gsum[at, :] + mm_nt(message_grad, w_middle[...])).astype(BF16)

    loop(m_blocks, middle_grad)
    mg_slots[r] = (mm_tn(m_low[...], m_gmsg[...]) * (m_rows * n_row) ** (-0.5)).astype(BF16)
    sum_middle.start()

    def fine_grad_pick(j):
        at = pl.ds(pl.multiple_of(j * wide, wide), wide)
        grad = cot[at, :].astype(F32) + p2 * mm(pick_map[at, :], table[...])
        grad_hidden[at, :] = grad
        grad = (grad * slope[at, :]).astype(BF16)
        grad_blocks[pl.ds(j * pair, pair)] = grad.reshape(pair, bs, width)

    loop(rows // wide, fine_grad_pick)

    f_count = fine_kind.shape[0]

    def fine_back(t):
        chain[t + 1] = mm(bank_t[fine_kind[t]], grad_blocks[fine_target[t]]) + chain[link[3, t]]

    loop(f_count, fine_back, UNROLL)
    for k in range(4):
        for i in range(send):
            back_fine[k, i] = chain[link[5, blocks + k * send + i]].astype(BF16)
    for item in home:
        item.start()
    sum_middle.wait()
    weight_out[1] = sum_middle.total()
    for item in home:
        item.wait()
    for k in range(4):
        for i in range(send):
            t = k * send + i
            chain[f_count + t + 1] = home_fine[k, i].astype(F32) + chain[link[4, t]]

    def fine_message_grad(b):
        at = pl.ds(pl.multiple_of(b * bs, bs), bs)
        grad_sum[at, :] = chain[link[5, b]].astype(BF16)

    loop(blocks, fine_message_grad)
    scale = (rows * n_row * n_col) ** (-0.5)
    fg_slots_col[c] = (mm_tn(feat[...], grad_sum[...]) * scale).astype(BF16)
    sum_fine_col.start()

    def fine_final(b):
        at = pl.ds(pl.multiple_of(b * bs, bs), bs)
        grad_out[at, :] = (grad_hidden[at, :] + mm_nt(grad_sum[at, :], w_fine[...])).astype(BF16)

    loop(blocks // 2, fine_final)
    sum_fine_col.wait()
    fg_slots_row[r] = sum_fine_col.total().astype(BF16)
    sum_fine_row.start()
    loop(blocks // 2, lambda b: fine_final(b + blocks // 2))
    sum_fine_row.wait()
    weight_out[0] = sum_fine_row.total()


def write_out(*refs):
    copies = [
        pltpu.make_async_copy(refs[k], refs[3 + k], refs[6].at[k]) for k in range(3)
    ]
    for copy in copies:
        copy.start()
    for copy in copies:
        copy.wait()


def local(
    features,
    cotangent,
    fine_weight,
    middle_weight,
    top_weight,
    tile_bank,
    fine_source,
    fine_target,
    fine_kind,
    tile_count,
    fine_sends,
    fine_pool,
    middle_source,
    middle_target,
    middle_kind,
    middle_sends,
    middle_pool,
    top_source,
    top_kind,
):
    n_row = lax.axis_size("row")
    n_col = lax.axis_size("col")
    bs = tile_bank.shape[1]
    kinds = tile_bank.shape[0]
    rows, width = features.shape
    blocks = rows // bs
    send = fine_sends.shape[0] // 4
    m_rows = middle_pool.shape[0]
    m_blocks = m_rows // bs
    m_send = middle_sends.shape[0] // 2
    t_slots = top_source.shape[0] // n_col
    chunk = m_rows // n_col
    f_count = fine_kind.shape[0]
    length = f_count + 4 * send
    def block_buf(*lead):
        return pltpu.VMEM(lead + (bs, width), BF16)

    def wide_buf(count, dtype):
        return pltpu.VMEM((count, width), dtype)

    part = pltpu.VMEM((n_col, chunk, width), BF16)
    n_sem = 12 + 8 * n_col + 4 * n_row
    arrays = [
        features,
        cotangent,
        fine_weight,
        middle_weight,
        top_weight,
        tile_bank,
        fine_pool.reshape(blocks, bs),
        middle_pool.reshape(m_blocks, bs),
    ] + [
        key.reshape(1, key.shape[0])
        for key in (
            fine_target,
            fine_source,
            fine_sends,
            middle_target,
            middle_source,
            middle_sends,
            top_source,
        )
    ]
    scratch = [pltpu.VMEM(array.shape, array.dtype) for array in arrays] + [
        block_buf(kinds),
        pltpu.VMEM((m_rows, rows), BF16),
        pltpu.VMEM((rows, m_rows), BF16),
        pltpu.VMEM((length + 1, bs, width), F32),
        block_buf(blocks + 4 * send),
        block_buf(4, send),
        block_buf(4, send),
        block_buf(4, send),
        wide_buf(rows, F32),
        wide_buf(rows, F32),
        wide_buf(rows, F32),
        wide_buf(rows, BF16),
        block_buf(blocks),
        part,
        part,
        part,
        part,
        part,
        part,
        block_buf(m_blocks + 2 * m_send),
        block_buf(2, m_send),
        block_buf(2, m_send),
        block_buf(2, m_send),
        wide_buf(m_rows, F32),
        wide_buf(m_rows, F32),
        block_buf(m_blocks),
        wide_buf(m_rows, BF16),
        wide_buf(m_rows, F32),
        wide_buf(m_rows, BF16),
        wide_buf(m_rows, BF16),
        block_buf(n_row),
        block_buf(n_row),
        block_buf(n_col),
        block_buf(n_col),
        block_buf(n_col),
        block_buf(n_col),
        wide_buf(n_col * bs, BF16),
        pltpu.VMEM((n_col * bs, 2 * width), BF16),
        block_buf(n_row),
        block_buf(n_col),
        block_buf(n_row),
        pltpu.VMEM((bs, m_rows), BF16),
        pltpu.VMEM((m_rows, n_col * bs), BF16),
        pltpu.VMEM((16, bs), jnp.int32),
        pltpu.VMEM((16, bs), jnp.int32),
        pltpu.SMEM((16, bs), jnp.int32),
        pltpu.SemaphoreType.DMA((len(arrays) + 1,)),
        pltpu.SemaphoreType.DMA((n_sem,)),
        pltpu.SemaphoreType.DMA((n_sem,)),
    ]
    smem = pl.BlockSpec(memory_space=pltpu.SMEM)
    vmem = pl.BlockSpec(memory_space=pltpu.VMEM)
    results = pl.pallas_call(
        functools.partial(kernel, (n_row, n_col, send, m_send, t_slots)),
        out_shape=(
            jax.ShapeDtypeStruct((rows, width), BF16),
            jax.ShapeDtypeStruct((rows, width), BF16),
            jax.ShapeDtypeStruct((3, width, width), F32),
        ),
        in_specs=[smem] * 11 + [pl.BlockSpec(memory_space=pltpu.HBM)] * len(arrays),
        out_specs=(vmem, vmem, vmem),
        scratch_shapes=scratch,
        compiler_params=pltpu.CompilerParams(
            collective_id=0, has_side_effects=True, vmem_limit_bytes=48 * 1024 * 1024
        ),
        cost_estimate=pl.CostEstimate(
            flops=4_000_000_000, bytes_accessed=4_000_000, transcendentals=400_000
        ),
    )(
        tile_count,
        fine_source,
        fine_target,
        fine_kind,
        fine_sends,
        middle_source,
        middle_target,
        middle_kind,
        middle_sends,
        top_source,
        top_kind,
        *arrays,
    )
    return pl.pallas_call(
        write_out,
        out_shape=[jax.ShapeDtypeStruct(x.shape, x.dtype) for x in results],
        in_specs=[pl.BlockSpec(memory_space=pl.ANY)] * 3,
        out_specs=[pl.BlockSpec(memory_space=pltpu.HBM)] * 3,
        scratch_shapes=[pltpu.SemaphoreType.DMA((3,))],
    )(*results)


def solution(mesh):
    everywhere = P(("group", "row", "col"))
    by_row = P(("group", "row"))
    in_specs = (
        (P(("group", "row", "col"), None),) * 2
        + (P(),) * 4
        + (everywhere,) * 6
        + (by_row,) * 5
        + (P("group"),) * 2
    )
    out_specs = (
        P(("group", "row", "col"), None),
        P(("group", "row", "col"), None),
        P("group", None, None),
    )
    return jax.shard_map(local, mesh=mesh, in_specs=in_specs, out_specs=out_specs, check_vma=False)
```
